256 devices in a mesh: gx: 16 (over y, x_lo, core), gy: 16 (over z, x_hi).
Axes of the slice: x: 4 (x_hi: 2, x_lo: 2; x = x_hi * 2 + x_lo), y: 4, z: 8, core: 2. Of those that a mesh axis runs over, the one named last changes fastest.
Arguments:
- tokens: bfloat16 [131072, 6144], P(('gx', 'gy')), may hold values from -24 to 24
- cotangent: bfloat16 [131072, 6144], P(('gx', 'gy')), may hold values from -0.0625 to 0.0625
- weights: float32 [6144, 512], P(('gx', 'gy')), may hold values from -1 to 1
- first_moment: float32 [6144, 512], P(('gx', 'gy')), may hold values from -0.012 to 0.012
- second_moment: float32 [6144, 512], P(('gx', 'gy')), may hold values from 1e-06 to 0.0001
- norm_gain: float32 [6144], P(('gx', 'gy')), may hold values from 0.5 to 1.5
- gain_first: float32 [6144], P(('gx', 'gy')), may hold values from -3 to 3
- gain_second: float32 [6144], P(('gx', 'gy')), may hold values from 0.05 to 5
Outputs:
- new_weights: float32 [6144, 512], P(('gx', 'gy'))
- new_first: float32 [6144, 512], P(('gx', 'gy'))
- new_second: float32 [6144, 512], P(('gx', 'gy'))
- new_gain: float32 [6144], P(('gx', 'gy'))
- new_gain_first: float32 [6144], P(('gx', 'gy'))
- new_gain_second: float32 [6144], P(('gx', 'gy'))
- next_weights: bfloat16 [6144, 512], replicated
- next_gain: bfloat16 [6144], replicated
The draws below stay inside these ranges and needn't reach their ends.
All inputs are finite; a program needn't handle non-finite values.
Results may differ from the reference program's by a relative error of at most 0.007.
The reference program's roundings to bfloat16 on the way (of `normed`, `attention_low`, `attended`, `grad_attended`, `grad_value` and `grad_scores`) count: a program that leaves them out, or rounds other values in their place, can miss the bound.
Values may be sent and summed in bfloat16 or wider, within the bound.
A program may use at most 128 MiB of HBM per device.

```python
import math
import jax
import jax.numpy as jnp
from jax import lax

D = 6144
HD = 128
IMG_TOK = 256
TOKENS = 131072


def draw_weights(key, part):
    key = jax.random.fold_in(key, 7)
    base = jax.random.truncated_normal(key, -4.0, 4.0, (D, 4 * HD), jnp.float32)
    return base * (0.25 * D ** (-0.5))


def strengthened(entries, rng, source, target, parts, factor):
    def block_of(position):
        return (jnp.arange(entries.shape[position]) // (entries.shape[position] // parts)).reshape((-1,) + (1,) * (entries.ndim - 1 - position))

    near = jax.random.permutation(rng, parts)[block_of(target)]
    far = (block_of(target) + parts // 2) % parts
    return jnp.where((block_of(source) == near) | (block_of(source) == far), factor * entries, entries)


def shard_levels(rng, dims, cuts, smallest, top_value):
    factor_of = 1.0
    for position, parts in cuts:
        heights = jax.random.uniform(jax.random.fold_in(jax.random.fold_in(rng, 6), position), (parts,), jnp.float32, smallest / len(cuts), top_value / len(cuts))
        factor_of = factor_of * jnp.repeat(jnp.exp(heights), dims[position] // parts).reshape((-1,) + (1,) * (len(dims) - 1 - position))
    return factor_of


def scatter_about(own_key, dims, scale, bound, pieces=(), held_as=jnp.bfloat16):
    array = jax.random.normal(own_key, dims, jnp.float32) * scale
    if len(pieces) > 0:
        array = shard_levels(own_key, dims, pieces, -0.22, 0.18) * array
    return jnp.clip(array, min=-bound, max=bound).astype(held_as)


def heavy_noise(own_key, extent, spread, limit, split, heavy, kind=jnp.bfloat16):
    result = spread * jax.random.normal(own_key, extent, jnp.float32)
    if split:
        result = result * shard_levels(own_key, extent, split, -0.22, 0.18)
    return jnp.clip(strengthened(result, jax.random.fold_in(own_key, 3), *heavy), -limit, limit).astype(kind)


def setup_inputs(seed: int = 0) -> dict:
    keys = jax.random.split(jax.random.key(seed), 9)
    return {
        "tokens": heavy_noise(keys[0], (TOKENS, D), 1.0, 24.0, ((0, 256),), (0, 1, 256, 6.0)),
        "cotangent": heavy_noise(keys[1], (TOKENS, D), TOKENS ** -0.5, 0.0625, ((0, 256),), (0, 1, 256, 6.0)),
        "weights": draw_weights(jax.random.fold_in(keys[8], 71), 0),
        "first_moment": scatter_about(keys[3], (D, 4 * HD), 0.003, 0.012, ((0, 256),), jnp.float32),
        "second_moment": jnp.clip(jnp.exp(math.log(0.0001) - 4.6051702 * jax.random.uniform(keys[4], (D, 4 * HD), jnp.float32) ** shard_levels(keys[4], (D, 4 * HD), ((0, 256),), -0.2, 0.2)), 9.999999974752427e-07, 0.0001),
        "norm_gain": jnp.clip(1.0 + 0.1 * jax.random.normal(keys[5], (D,), jnp.float32), 0.5, 1.5),
        "gain_first": scatter_about(keys[6], (D,), 0.5, 3.0, ((0, 256),), jnp.float32),
        "gain_second": jnp.clip(jnp.exp(math.log(5.0) - 4.6051702 * jax.random.uniform(keys[7], (D,), jnp.float32) ** shard_levels(keys[7], (D,), ((0, 256),), -0.2, 0.2)), 0.05, 5.0),
    }


EPS_NORM = 1e-06
BETA_ONE = 0.9
BETA_TWO = 0.95
LEARN_RATE = 0.001
DECAY_RATE = 0.1
ADAM_EPS = 1e-08
CORRECT_ONE = 1.0 - 0.9 ** 10
CORRECT_TWO = 1.0 - 0.95 ** 10

def normalize(values):
    average = lax.optimization_barrier(jnp.mean(values, axis=-1, keepdims=True))
    centred = values - average
    inverse = lax.rsqrt(lax.optimization_barrier(jnp.mean(centred * centred, axis=-1, keepdims=True)) + EPS_NORM)
    return (centred * inverse, inverse)

def norm_back(grad_hat, normed, inverse):
    first_part = lax.optimization_barrier(jnp.mean(grad_hat, axis=-1, keepdims=True))
    second_part = normed * lax.optimization_barrier(jnp.mean(grad_hat * normed, axis=-1, keepdims=True))
    return inverse * (grad_hat - first_part - second_part)

def batched(form, left, right):
    return jnp.einsum(form, left.astype(jnp.float32), right.astype(jnp.float32), precision=lax.Precision.HIGHEST)

def block_terms(images, tangent, low_weights, low_gain):
    count_img, seq_len, features = images.shape
    head_dim = low_weights.shape[1] // 4
    flattened = images.reshape(count_img * seq_len, features).astype(jnp.float32)
    standard, ignored = normalize(flattened)
    normed = (standard * low_gain.astype(jnp.float32)).astype(jnp.bfloat16)
    projected = jnp.dot(normed, low_weights[:, :3 * head_dim], preferred_element_type=jnp.float32)
    query_hat, query_inverse = normalize(projected[:, :head_dim])
    key_hat, key_inverse = normalize(projected[:, head_dim:2 * head_dim])
    query_low = query_hat.astype(jnp.bfloat16).reshape(count_img, seq_len, head_dim)
    key_low = key_hat.astype(jnp.bfloat16).reshape(count_img, seq_len, head_dim)
    value_low = projected[:, 2 * head_dim:].astype(jnp.bfloat16).reshape(count_img, seq_len, head_dim)
    scaling = head_dim ** (-0.5)
    scores = batched('nsh,nth->nst', query_low, key_low) * scaling
    exponent = jnp.exp(scores)
    attention = exponent / lax.optimization_barrier(jnp.sum(exponent, axis=-1, keepdims=True))
    attention_low = attention.astype(jnp.bfloat16)
    attended = batched('nst,nth->nsh', attention_low, value_low).astype(jnp.bfloat16)
    attended = attended.reshape(count_img * seq_len, head_dim)
    tangent_flat = tangent.reshape(count_img * seq_len, features)
    grad_out = lax.dot_general(tangent_flat, attended, (((0,), (0,)), ((), ())), preferred_element_type=jnp.float32)
    grad_attended = jnp.dot(tangent_flat, low_weights[:, 3 * head_dim:], preferred_element_type=jnp.float32)
    grad_attended = grad_attended.astype(jnp.bfloat16).reshape(count_img, seq_len, head_dim)
    grad_value = batched('nst,nsh->nth', attention_low, grad_attended).astype(jnp.bfloat16)
    grad_attention = batched('nsh,nth->nst', grad_attended, value_low)
    row_total = lax.optimization_barrier(jnp.sum(attention * grad_attention, axis=-1, keepdims=True))
    grad_scores = (attention * (grad_attention - row_total) * scaling).astype(jnp.bfloat16)
    grad_query_hat = batched('nst,nth->nsh', grad_scores, key_low).reshape(count_img * seq_len, head_dim)
    grad_key_hat = batched('nst,nsh->nth', grad_scores, query_low).reshape(count_img * seq_len, head_dim)
    grad_query = norm_back(grad_query_hat, query_hat, query_inverse).astype(jnp.bfloat16)
    grad_key = norm_back(grad_key_hat, key_hat, key_inverse).astype(jnp.bfloat16)
    grad_proj = jnp.concatenate([grad_query, grad_key, grad_value.reshape(count_img * seq_len, head_dim)], axis=1)
    grad_in = lax.dot_general(normed, grad_proj, (((0,), (0,)), ((), ())), preferred_element_type=jnp.float32)
    grad_normed = lax.dot_general(grad_proj, low_weights[:, :3 * head_dim], (((1,), (1,)), ((), ())), preferred_element_type=jnp.float32)
    grad_gain = lax.optimization_barrier(jnp.sum(grad_normed * standard, axis=0))
    return (jnp.concatenate([grad_in, grad_out], axis=1), grad_gain)

def adam_step(parameter, moment_one, moment_two, gradient, decay_rate):
    fresh_one = BETA_ONE * moment_one + (1.0 - BETA_ONE) * gradient
    fresh_two = BETA_TWO * moment_two + (1.0 - BETA_TWO) * gradient * gradient
    adjusted = fresh_one / CORRECT_ONE / (jnp.sqrt(fresh_two / CORRECT_TWO) + ADAM_EPS)
    return (parameter - LEARN_RATE * (adjusted + decay_rate * parameter), fresh_one, fresh_two)

def reference(tokens, cotangent, weights, first_moment, second_moment, norm_gain, gain_first, gain_second):
    low_weights = weights.astype(jnp.bfloat16)
    low_gain = norm_gain.astype(jnp.bfloat16)
    images = tokens.reshape(TOKENS // IMG_TOK, IMG_TOK, D)
    tangents = cotangent.reshape(TOKENS // IMG_TOK, IMG_TOK, D)

    def accumulate(carry, pair):
        term_weights, term_gain = block_terms(pair[0][None], pair[1][None], low_weights, low_gain)
        return ((carry[0] + term_weights, carry[1] + term_gain), None)
    start = (jnp.zeros((D, 4 * HD), jnp.float32), jnp.zeros((D,), jnp.float32))
    totals, ignored = lax.scan(accumulate, start, (images, tangents))
    new_weights, new_first, new_second = adam_step(weights, first_moment, second_moment, totals[0], DECAY_RATE)
    new_gain, new_gain_first, new_gain_second = adam_step(norm_gain, gain_first, gain_second, totals[1], 0.0)
    return (new_weights, new_first, new_second, new_gain, new_gain_first, new_gain_second, new_weights.astype(jnp.bfloat16), new_gain.astype(jnp.bfloat16))
```

```python
import functools

import jax
import jax.numpy as jnp
from jax import lax
from jax.experimental import pallas as pl
from jax.experimental.pallas import tpu as pltpu
from jax.sharding import PartitionSpec as P

IMG_TOK = 256
EPS_NORM = 1e-06
BETA_ONE = 0.9
BETA_TWO = 0.95
LEARN_RATE = 0.001
DECAY_RATE = 0.1
ADAM_EPS = 1e-08
CORRECT_ONE = 1.0 - 0.9**10
CORRECT_TWO = 1.0 - 0.95**10
MESH = pl.DeviceIdType.MESH
BF16, F32 = jnp.bfloat16, jnp.float32

VIEW = (2, 2, 2, 2, 4, 2, 48, 512)
GVIEW = (2, 2, 2, 2, 4, 2, 2, 1, 128)
FAR = [(dy, dz, dx) for dy in range(2) for dz in range(4) for dx in range(2)][1:]
ORDERS = (("z", "y", "x"), ("x", "z", "y"), ("y", "x", "z"))


class Place:
    def __init__(self):
        gx, gy = lax.axis_index("gx"), lax.axis_index("gy")
        self.y, self.z = gx // 4, gy // 2
        self.xl, self.c, self.xh = lax.rem(gx // 2, 2), lax.rem(gx, 2), lax.rem(gy, 2)
        self.yh, self.yl, self.zf, self.zl = self.y // 2, lax.rem(self.y, 2), self.z // 2, lax.rem(self.z, 2)
        self.x = self.xh * 2 + self.xl
        self.low = {"x": self.xl, "y": self.yl, "z": self.zl}

    def device(self, x, y, z, c):
        return (y * 4 + lax.rem(x, 2) * 2 + c, z * 2 + x // 2)

    def step(self, axis, by):
        x, y, z = self.x, self.y, self.z
        if axis == "x":
            x = lax.rem(x + by + 4, 4)
        elif axis == "y":
            y = lax.rem(y + by + 4, 4)
        else:
            z = lax.rem(z + by + 8, 8)
        return self.device(x, y, z, self.c)

    def sibling(self):
        return self.device(self.x, self.y, self.z, 1 - self.c)

    def far(self, offset):
        dy, dz, dx = offset
        yh, zf, xh = lax.rem(self.yh + dy, 2), lax.rem(self.zf + dz, 4), lax.rem(self.xh + dx, 2)
        return yh, zf, xh, self.device(xh * 2 + self.xl, yh * 2 + self.yl, zf * 2 + self.zl, self.c)


def enter(me):
    barrier = pltpu.get_barrier_semaphore()
    others = [me.far(f)[3] for f in FAR] + [me.step(a, b) for a in "xyz" for b in (1, -1)] + [me.sibling()]
    for other in others:
        pl.semaphore_signal(barrier, inc=1, device_id=other, device_id_type=MESH)
    pl.semaphore_wait(barrier, len(others))


def gather_kernel(shard, gain, full, gfull, land, fs, fr, gs, gr, ns, nr, ss, sr):
    me = Place()
    enter(me)
    own = (me.yh * 4 + me.zf) * 2 + me.xh
    gplace = gfull.at[me.yh, me.yl, me.xl, me.c, me.zf, me.zl, me.xh]
    gplace[...] = gain[...]
    sends = []

    def push(src, dst, ssem, rsem, to):
        copy = pltpu.make_async_remote_copy(src, dst, ssem, rsem, device_id=to, device_id_type=MESH)
        copy.start()
        sends.append(copy)
        return copy

    far = []
    for k, f in enumerate(FAR):
        to = me.far(f)[3]
        far.append(push(shard, land.at[own], fs.at[k], fr.at[k], to))
        far.append(push(gplace, gplace, gs.at[k], gr.at[k], to))
    land[own] = shard[...]
    for copy in far:
        copy.wait_recv()
    for yh in range(2):
        for zf in range(4):
            a, b = (land[(yh * 4 + zf) * 2 + xh].astype(F32) for xh in range(2))
            block = jnp.concatenate(
                [jnp.concatenate([a[:24], b[:24]], 0), jnp.concatenate([a[24:], b[24:]], 0)], 1
            )
            full[yh, me.yl, me.xl, me.c, zf, me.zl] = block.astype(BF16)

    def part(ref, done, half, p):
        at = {a: (slice(None) if a in done else me.low[a]) for a in "xyz"}
        rows = slice(None) if p is None else pl.ds(16 * p, 16)
        return ref.at[half, at["y"], at["x"], me.c, :, at["z"], rows]

    def fresh(ref, done, axis, half, p):
        at = {a: (slice(None) if a in done else me.low[a]) for a in "xyz"}
        at[axis] = 1 - me.low[axis]
        rows = slice(None) if p is None else pl.ds(16 * p, 16)
        return ref.at[half, at["y"], at["x"], me.c, :, at["z"], rows]

    shared = []
    count = [0]

    def share(ref):
        k = count[0]
        count[0] += 1
        shared.append(push(ref, ref, ss.at[k], sr.at[k], me.sibling()))

    def near(stage, p):
        order = ORDERS[p]
        axis, done = order[stage], order[:stage]
        k = (stage * 3 + p) * 2
        copies = []
        for half in range(2):
            src = part(full, done, half, p)
            copies.append(push(src, src, ns.at[k + half], nr.at[k + half], me.step(axis, 1 - 2 * half)))
        return copies

    def near_gain(stage):
        axis, done = "zyx"[stage], "zyx"[:stage]
        at = {a: (slice(None) if a in done else me.low[a]) for a in "xyz"}
        src = gfull.at[:, at["y"], at["x"], me.c, :, at["z"]]
        return push(src, src, ns.at[18 + stage], nr.at[18 + stage], me.step(axis, 1))

    flight = [near(0, p) for p in range(3)]
    gflight = near_gain(0)
    share(full.at[:, me.yl, me.xl, me.c, :, me.zl])
    for stage in range(3):
        later = []
        for p in range(3):
            for copy in flight[p]:
                copy.wait_recv()
            if stage < 2:
                later.append(near(stage + 1, p))
            for half in range(2):
                share(fresh(full, ORDERS[p][:stage], ORDERS[p][stage], half, p))
        gflight.wait_recv()
        if stage < 2:
            gflight = near_gain(stage + 1)
        flight = later
    share(gfull.at[:, :, :, me.c])
    for copy in shared:
        copy.wait_recv()
    for copy in sends:
        copy.wait_send()


def gather_all(low_rows, low_gain, ident):
    shard = jnp.concatenate([low_rows[:, :256], low_rows[:, 256:]], axis=0)
    gain = jnp.pad(low_gain.astype(F32), (0, 104)).reshape(1, 128)
    dma = pltpu.SemaphoreType.DMA
    full, gfull = pl.pallas_call(
        gather_kernel,
        name="gather%d" % ident,
        out_shape=(jax.ShapeDtypeStruct(VIEW, BF16), jax.ShapeDtypeStruct(GVIEW, F32)),
        in_specs=[pl.BlockSpec(memory_space=pltpu.VMEM)] * 2,
        out_specs=(pl.BlockSpec(memory_space=pltpu.VMEM),) * 2,
        scratch_shapes=[
            pltpu.VMEM((16, 48, 256), BF16),
            dma((15,)), dma((15,)), dma((15,)), dma((15,)),
            dma((21,)), dma((21,)), dma((20,)), dma((20,)),
        ],
        compiler_params=pltpu.CompilerParams(
            collective_id=ident, has_side_effects=True, vmem_limit_bytes=40 << 20
        ),
    )(shard, gain)
    return full.reshape(6144, 512), gfull.reshape(256, 128)[:, :24].reshape(6144).astype(BF16)


def scatter_kernel(grad, out, acc, sib_out, sib_in, nout, nin, fout, fin, bs, br, ns, nr, fs, fr, load):
    me = Place()
    big = pltpu.make_async_copy(grad, acc, load)
    big.start()
    enter(me)
    big.wait()
    sends = []

    def push(src, dst, ssem, rsem, to):
        copy = pltpu.make_async_remote_copy(src, dst, ssem, rsem, device_id=to, device_id_type=MESH)
        copy.start()
        sends.append(copy)
        return copy

    sib = []
    for yh in range(2):
        for yl in range(2):
            k = yh * 2 + yl

            def cast(i, carry):
                xl, zf = i // 4, lax.rem(i, 4)
                sib_out[yh, yl, xl, zf] = acc[yh, yl, xl, 1 - me.c, zf].astype(BF16)
                return carry

            lax.fori_loop(0, 8, cast, 0)
            sib.append(push(sib_out.at[yh, yl], sib_in.at[yh, yl], bs.at[k], br.at[k], me.sibling()))
    for yh in range(2):
        for yl in range(2):
            sib[yh * 2 + yl].wait_recv()

            def add(i, carry):
                xl, zf = i // 4, lax.rem(i, 4)
                acc[yh, yl, xl, me.c, zf] += sib_in[yh, yl, xl, zf].astype(F32)
                return carry

            lax.fori_loop(0, 8, add, 0)

    def combos(stage, p):
        order = ORDERS[p][::-1]
        axis, rest, gone = order[stage], order[stage + 1:], order[:stage]
        found = []
        for n in range(2 ** len(rest)):
            found.append({a: (n >> i) & 1 for i, a in enumerate(rest)} | {a: me.low[a] for a in gone})
        return axis, found

    def base(stage):
        return (0, 4, 6)[stage]

    def near(stage, p):
        axis, found = combos(stage, p)
        copies = []
        for half in range(2):
            for n, at in enumerate(found):
                yl, xl, zl = ((1 - me.low[a]) if a == axis else at[a] for a in "yxz")
                nout[p, half, base(stage) + n] = acc[
                    half, yl, xl, me.c, :, zl, pl.ds(16 * p, 16), :
                ].astype(BF16)
            where = (p, half, pl.ds(base(stage), len(found)))
            k = (stage * 3 + p) * 2 + half
            copies.append(push(nout.at[where], nin.at[where], ns.at[k], nr.at[k], me.step(axis, 1 - 2 * half)))
        return copies

    def near_add(stage, p, copies):
        axis, found = combos(stage, p)
        for half in range(2):
            copies[half].wait_recv()
            for n, at in enumerate(found):
                yl, xl, zl = (me.low[a] if a == axis else at[a] for a in "yxz")
                place = (half, yl, xl, me.c, slice(None), zl, pl.ds(16 * p, 16), slice(None))
                acc[place] = acc[place] + nin[p, half, base(stage) + n].astype(F32)

    flight = [near(0, p) for p in range(3)]
    for stage in range(3):
        later = []
        for p in range(3):
            near_add(stage, p, flight[p])
            if stage < 2:
                later.append(near(stage + 1, p))
        flight = later

    def mine(yh, zf, xh):
        block = acc[yh, me.yl, me.xl, me.c, zf, me.zl]
        return block[:24] if xh == 0 else block[24:]

    for yh in range(2):
        for zf in range(4):
            for xh in range(2):
                rows = mine(yh, zf, xh)
                fout[(yh * 4 + zf) * 2 + xh] = jnp.concatenate([rows[:, :256], rows[:, 256:]], 0)
    fcopies = []
    for k, f in enumerate(FAR):
        yh, zf, xh, to = me.far(f)
        fcopies.append(push(fout.at[(yh * 4 + zf) * 2 + xh], fin.at[k], fs.at[k], fr.at[k], to))
    total = fout[(me.yh * 4 + me.zf) * 2 + me.xh]
    for k in range(15):
        fcopies[k].wait_recv()
        total = total + fin[k]
    out[:, :256] = total[:24]
    out[:, 256:] = total[24:]
    for copy in sends:
        copy.wait_send()


def scatter_sum(grad, ident):
    dma = pltpu.SemaphoreType.DMA
    return pl.pallas_call(
        scatter_kernel,
        name="scatter%d" % ident,
        out_shape=jax.ShapeDtypeStruct((24, 512), F32),
        in_specs=[pl.BlockSpec(memory_space=pl.ANY)],
        out_specs=pl.BlockSpec(memory_space=pltpu.VMEM),
        scratch_shapes=[
            pltpu.VMEM((2, 2, 2, 2, 4, 2, 48, 512), F32),
            pltpu.VMEM((2, 2, 2, 4, 2, 48, 512), BF16),
            pltpu.VMEM((2, 2, 2, 4, 2, 48, 512), BF16),
            pltpu.VMEM((3, 2, 7, 4, 16, 512), BF16),
            pltpu.VMEM((3, 2, 7, 4, 16, 512), BF16),
            pltpu.VMEM((16, 48, 256), F32),
            pltpu.VMEM((15, 48, 256), F32),
            dma((4,)), dma((4,)), dma((18,)), dma((18,)), dma((15,)), dma((15,)), dma(()),
        ],
        compiler_params=pltpu.CompilerParams(
            collective_id=ident, has_side_effects=True, vmem_limit_bytes=48 << 20
        ),
    )(grad.reshape(VIEW))


def normalize(values):
    average = jnp.mean(values, axis=-1, keepdims=True)
    centred = values - average
    inverse = lax.rsqrt(jnp.mean(centred * centred, axis=-1, keepdims=True) + EPS_NORM)
    return (centred * inverse, inverse)


def norm_back(grad_hat, normed, inverse):
    first_part = jnp.mean(grad_hat, axis=-1, keepdims=True)
    second_part = normed * jnp.mean(grad_hat * normed, axis=-1, keepdims=True)
    return inverse * (grad_hat - first_part - second_part)


def product(form, left, right):
    return jnp.einsum(form, left, right, preferred_element_type=jnp.float32)


def local_terms(tokens, cotangent, low_weights, low_gain):
    total_rows, features = tokens.shape
    count_img = total_rows // IMG_TOK
    head_dim = low_weights.shape[1] // 4
    standard, ignored = normalize(tokens.astype(jnp.float32))
    normed = (standard * low_gain.astype(jnp.float32)).astype(jnp.bfloat16)
    projected = jnp.dot(normed, low_weights[:, : 3 * head_dim], preferred_element_type=jnp.float32)
    query_hat, query_inverse = normalize(projected[:, :head_dim])
    key_hat, key_inverse = normalize(projected[:, head_dim : 2 * head_dim])
    query_low = query_hat.astype(jnp.bfloat16).reshape(count_img, IMG_TOK, head_dim)
    key_low = key_hat.astype(jnp.bfloat16).reshape(count_img, IMG_TOK, head_dim)
    value_low = (
        projected[:, 2 * head_dim :].astype(jnp.bfloat16).reshape(count_img, IMG_TOK, head_dim)
    )
    scaling = head_dim ** (-0.5)
    scores = product("nsh,nth->nst", query_low, key_low) * scaling
    exponent = jnp.exp(scores)
    attention = exponent / jnp.sum(exponent, axis=-1, keepdims=True)
    attention_low = attention.astype(jnp.bfloat16)
    attended = product("nst,nth->nsh", attention_low, value_low).astype(jnp.bfloat16)
    attended = attended.reshape(total_rows, head_dim)
    grad_out = lax.dot_general(
        cotangent, attended, (((0,), (0,)), ((), ())), preferred_element_type=jnp.float32
    )
    grad_attended = jnp.dot(
        cotangent, low_weights[:, 3 * head_dim :], preferred_element_type=jnp.float32
    )
    grad_attended = grad_attended.astype(jnp.bfloat16).reshape(count_img, IMG_TOK, head_dim)
    grad_value = product("nst,nsh->nth", attention_low, grad_attended).astype(jnp.bfloat16)
    grad_attention = product("nsh,nth->nst", grad_attended, value_low)
    row_total = jnp.sum(attention * grad_attention, axis=-1, keepdims=True)
    grad_scores = (attention * (grad_attention - row_total) * scaling).astype(jnp.bfloat16)
    grad_query_hat = product("nst,nth->nsh", grad_scores, key_low).reshape(total_rows, head_dim)
    grad_key_hat = product("nst,nsh->nth", grad_scores, query_low).reshape(total_rows, head_dim)
    grad_query = norm_back(grad_query_hat, query_hat, query_inverse).astype(jnp.bfloat16)
    grad_key = norm_back(grad_key_hat, key_hat, key_inverse).astype(jnp.bfloat16)
    grad_proj = jnp.concatenate(
        [grad_query, grad_key, grad_value.reshape(total_rows, head_dim)], axis=1
    )
    grad_in = lax.dot_general(
        normed, grad_proj, (((0,), (0,)), ((), ())), preferred_element_type=jnp.float32
    )
    return jnp.concatenate([grad_in, grad_out], axis=1)


def adam_step(parameter, moment_one, moment_two, gradient, decay_rate):
    fresh_one = BETA_ONE * moment_one + (1.0 - BETA_ONE) * gradient
    fresh_two = BETA_TWO * moment_two + (1.0 - BETA_TWO) * gradient * gradient
    adjusted = fresh_one / CORRECT_ONE / (jnp.sqrt(fresh_two / CORRECT_TWO) + ADAM_EPS)
    return (parameter - LEARN_RATE * (adjusted + decay_rate * parameter), fresh_one, fresh_two)


def shards(
    tokens, cotangent, weights, first_moment, second_moment, norm_gain, gain_first, gain_second
):
    low_weights = weights.astype(jnp.bfloat16)
    low_gain = norm_gain.astype(jnp.bfloat16)
    full_weights, full_gain = gather_all(low_weights, low_gain, 1)
    terms = local_terms(tokens, cotangent, full_weights, full_gain)
    grad_weights = scatter_sum(terms, 2)
    grad_gain = jnp.sum(
        grad_weights[:, :384] * low_weights[:, :384].astype(F32), axis=1
    ) / low_gain.astype(F32)
    new_weights, new_first, new_second = adam_step(
        weights, first_moment, second_moment, grad_weights, DECAY_RATE
    )
    new_gain, new_gain_first, new_gain_second = adam_step(
        norm_gain, gain_first, gain_second, grad_gain, 0.0
    )
    next_weights, next_gain = gather_all(
        new_weights.astype(jnp.bfloat16), new_gain.astype(jnp.bfloat16), 3
    )
    return (
        new_weights,
        new_first,
        new_second,
        new_gain,
        new_gain_first,
        new_gain_second,
        next_weights,
        next_gain,
    )


def solution(mesh):
    rows, line = P(("gx", "gy"), None), P(("gx", "gy"))
    return jax.shard_map(
        shards,
        mesh=mesh,
        in_specs=(rows,) * 5 + (line,) * 3,
        out_specs=(rows,) * 3 + (line,) * 3 + (P(), P()),
        check_vma=False,
    )
```

```python
import functools

import jax
import jax.numpy as jnp
from jax import lax
from jax.experimental import pallas as pl
from jax.experimental.pallas import tpu as pltpu
from jax.sharding import PartitionSpec as P

IMG_TOK = 256
EPS_NORM = 1e-06
BETA_ONE = 0.9
BETA_TWO = 0.95
LEARN_RATE = 0.001
DECAY_RATE = 0.1
ADAM_EPS = 1e-08
CORRECT_ONE = 1.0 - 0.9**10
CORRECT_TWO = 1.0 - 0.95**10
MESH = pl.DeviceIdType.MESH
BF16, F32 = jnp.bfloat16, jnp.float32

VIEW = (2, 2, 2, 2, 4, 2, 48, 512)
GVIEW = (2, 2, 2, 2, 4, 2, 2, 1, 128)
ROWS, HEAD, CHUNK = 512, 128, 384
FAR_Z = [(0, dz, 0) for dz in (1, 3, 2)]
FAR_XY = [(0, 0, 1), (1, 0, 0), (1, 0, 1)]
EARLY, LATE = pl.ds(0, 32), pl.ds(32, 16)
ORDERS = (("z", "y", "x"), ("x", "z", "y"), ("y", "x", "z"))


class Place:
    def __init__(self):
        gx, gy = lax.axis_index("gx"), lax.axis_index("gy")
        self.y, self.z = gx // 4, gy // 2
        self.xl, self.c, self.xh = lax.rem(gx // 2, 2), lax.rem(gx, 2), lax.rem(gy, 2)
        self.yh, self.yl, self.zf, self.zl = self.y // 2, lax.rem(self.y, 2), self.z // 2, lax.rem(self.z, 2)
        self.x = self.xh * 2 + self.xl
        self.low = {"x": self.xl, "y": self.yl, "z": self.zl}

    def device(self, x, y, z, c):
        return (y * 4 + lax.rem(x, 2) * 2 + c, z * 2 + x // 2)

    def step(self, axis, by):
        x, y, z = self.x, self.y, self.z
        if axis == "x":
            x = lax.rem(x + by + 4, 4)
        elif axis == "y":
            y = lax.rem(y + by + 4, 4)
        else:
            z = lax.rem(z + by + 8, 8)
        return self.device(x, y, z, self.c)

    def sibling(self):
        return self.device(self.x, self.y, self.z, 1 - self.c)

    def far(self, offset):
        dy, dz, dx = offset
        yh, zf, xh = lax.rem(self.yh + dy, 2), lax.rem(self.zf + dz, 4), lax.rem(self.xh + dx, 2)
        return yh, zf, xh, self.device(xh * 2 + self.xl, yh * 2 + self.yl, zf * 2 + self.zl, self.c)


def enter(me):
    barrier = pltpu.get_barrier_semaphore()
    others = [me.far(f)[3] for f in FAR_Z + FAR_XY] + [me.step(a, b) for a in "xyz" for b in (1, -1)] + [me.sibling()]
    for other in others:
        pl.semaphore_signal(barrier, inc=1, device_id=other, device_id_type=MESH)
    pl.semaphore_wait(barrier, len(others))


class Mail:
    def __init__(self):
        self.sends = []

    def push(self, src, dst, ssem, rsem, to):
        copy = pltpu.make_async_remote_copy(src, dst, ssem, rsem, device_id=to, device_id_type=MESH)
        copy.start()
        self.sends.append(copy)
        return copy

    def close(self):
        for copy in self.sends:
            copy.wait_send()


def gather(me, mail, shard, full, gfull, land, sems, between, result=None, rsem=None):
    fs, fr, gs, gr, ns, nr, ss, sr = sems
    yh, zf, xh = me.yh, me.zf, me.xh
    land[yh, zf, xh] = shard[...]

    def far(first, src_z, src_xy):
        copies = []
        for group, src in ((FAR_Z, src_z), (FAR_XY, src_xy)):
            for f in group:
                k = first + len(copies)
                copies.append(mail.push(src, src, fs.at[k], fr.at[k], me.far(f)[3]))
        return copies

    def far_gain(first, group, src):
        return [
            mail.push(src, src, gs.at[first + k], gr.at[first + k], me.far(f)[3]) for k, f in enumerate(group)
        ]

    own_gain = gfull.at[:, me.yl, me.xl, me.c, :, me.zl]
    gains = far_gain(0, FAR_Z, own_gain.at[yh, zf, xh])
    copies = far(0, land.at[yh, zf, xh, EARLY], land.at[yh, zf, xh, LATE])
    between[0]()
    for copy in gains:
        copy.wait_recv()
    gains = far_gain(3, FAR_XY, own_gain.at[yh, :, xh])
    for copy in copies:
        copy.wait_recv()
    copies = far(6, land.at[:, zf, :, LATE], land.at[yh, :, xh, EARLY])
    between[1]()
    for copy in gains + copies:
        copy.wait_recv()

    def near_gain(stage):
        axis, done = "zyx"[stage], "zyx"[:stage]
        at = {a: (slice(None) if a in done else me.low[a]) for a in "xyz"}
        src = gfull.at[:, at["y"], at["x"], me.c, :, at["z"]]
        return mail.push(src, src, gs.at[6 + stage], gr.at[6 + stage], me.step(axis, 1))

    gflight = near_gain(0)
    for h in range(2):
        for f in range(4):
            a, b = (land[h, f, g].astype(F32) for g in range(2))
            block = jnp.concatenate(
                [jnp.concatenate([a[:24], b[:24]], 0), jnp.concatenate([a[24:], b[24:]], 0)], 1
            )
            full[h, me.yl, me.xl, me.c, f, me.zl] = block.astype(BF16)

    def part(ref, done, half, zfar, p, fresh=None):
        at = {a: (slice(None) if a in done else me.low[a]) for a in "xyz"}
        if fresh is not None:
            at[fresh] = 1 - me.low[fresh]
        return ref.at[half, at["y"], at["x"], me.c, zfar, at["z"], pl.ds(16 * p, 16)]

    shared, local = [], []

    def share(view, src):
        k = len(shared)
        to = src if result is None else result
        shared.append(mail.push(view(src), view(to), ss.at[k], sr.at[k], me.sibling()))
        if result is not None:
            local.append(pltpu.make_async_copy(view(src), view(result), rsem.at[k]))
            local[-1].start()

    both = slice(None)
    flight = {}

    def near(stage, q):
        for p in range(3):
            axis, done = ORDERS[p][stage], ORDERS[p][:stage]
            for half in range(2):
                if stage > 0:
                    flight[stage - 1, p, half, q].wait_recv()
                src = part(full, done, half, pl.ds(2 * q, 2), p)
                k = ((stage * 3 + p) * 2 + half) * 2 + q
                flight[stage, p, half, q] = mail.push(src, src, ns.at[k], nr.at[k], me.step(axis, 1 - 2 * half))

    def spread_news(stage, zfar):
        for p in range(3):
            share(lambda ref: part(ref, ORDERS[p][:stage], both, zfar, p, ORDERS[p][stage]), full)

    near(0, 0)
    near(0, 1)
    share(lambda ref: ref.at[:, me.yl, me.xl, me.c, :, me.zl], full)
    between[2]()
    for stage in (1, 2):
        gflight.wait_recv()
        gflight = near_gain(stage)
        near(stage, 0)
        near(stage, 1)
        spread_news(stage - 1, both)
        between[2 + stage]()
    gflight.wait_recv()
    place = gfull.at[:, :, :, me.c]
    shared.append(mail.push(place, place, ss.at[7], sr.at[7], me.sibling()))
    between[5](shared[-1])
    for q in range(2):
        for p in range(3):
            for half in range(2):
                flight[2, p, half, q].wait_recv()
        spread_news(2, pl.ds(2 * q, 2))
    between[6]()
    for k, copy in enumerate(shared):
        if k != 7:
            copy.wait_recv()
    for copy in local:
        copy.wait()


def gain_rows(gfull):
    feature = lax.broadcasted_iota(jnp.int32, (128, CHUNK), 1).astype(F32)
    lane = lax.broadcasted_iota(jnp.int32, (128, CHUNK), 0).astype(F32)
    spread = jnp.where(feature - 24.0 * jnp.floor((feature + 0.5) * (1.0 / 24.0)) == lane, 1.0, 0.0).astype(BF16)
    feature = lax.broadcasted_iota(jnp.int32, (16, CHUNK), 1)
    source = lax.broadcasted_iota(jnp.int32, (16, CHUNK), 0)
    pick = jnp.where((feature >= 24 * source) & (feature < 24 * source + 24), 1.0, 0.0)
    flat = gfull[...].reshape(256, 128).astype(BF16)
    wide = jnp.dot(flat, spread, preferred_element_type=F32)
    return jnp.sum(wide.reshape(16, 16, CHUNK) * pick[None], axis=1)


def columns(j):
    return pl.ds(pl.multiple_of(j * CHUNK, 128), CHUNK)


def statistics(tok, mean, inverse, first, count):
    def rows(i, carry):
        at = pl.ds(pl.multiple_of(i * 16, 16), 16)
        values = tok[at, :].astype(F32)
        average = jnp.mean(values, axis=-1, keepdims=True)
        centred = values - average
        spread = jnp.mean(centred * centred, axis=-1, keepdims=True)
        mean[at, :] = average
        inverse[at, :] = lax.rsqrt(spread + EPS_NORM)
        return carry

    lax.fori_loop(first, first + count, rows, 0)


def scale_tokens(tok, gains, mean, inverse, c):
    def chunk(i, carry):
        j = i * 2 + c
        at = columns(j)
        standard = (tok[:, at].astype(F32) - mean[...]) * inverse[...]
        tok[:, at] = (standard * gains[pl.ds(j, 1), :]).astype(BF16)
        return carry

    lax.fori_loop(0, 8, chunk, 0)


def project(tok, cot, full, proj, c, first):
    at = [columns(i * 2 + c) for i in range(8)]
    low = full[:, :, :, c].reshape(8 * CHUNK, 4 * HEAD)
    inner = jnp.dot(jnp.concatenate([tok[:, a] for a in at], 1), low[:, : 3 * HEAD], preferred_element_type=F32)
    outer = jnp.dot(jnp.concatenate([cot[:, a] for a in at], 1), low[:, 3 * HEAD :], preferred_element_type=F32)
    if not first:
        inner, outer = inner + proj[:, : 3 * HEAD], outer + proj[:, 3 * HEAD :]
    proj[:, : 3 * HEAD] = inner
    proj[:, 3 * HEAD :] = outer


def normalize(values):
    average = jnp.mean(values, axis=-1, keepdims=True)
    centred = values - average
    inverse = lax.rsqrt(jnp.mean(centred * centred, axis=-1, keepdims=True) + EPS_NORM)
    return (centred * inverse, inverse)


def norm_back(grad_hat, normed, inverse):
    first_part = jnp.mean(grad_hat, axis=-1, keepdims=True)
    second_part = normed * jnp.mean(grad_hat * normed, axis=-1, keepdims=True)
    return inverse * (grad_hat - first_part - second_part)


def dot(left, right, dims):
    return lax.dot_general(left, right, (((dims[0],), (dims[1],)), ((), ())), preferred_element_type=F32)


def attend(proj, gproj):
    scaling = HEAD ** (-0.5)
    for image in range(ROWS // IMG_TOK):
        at = pl.ds(image * IMG_TOK, IMG_TOK)
        query_hat, query_inverse = normalize(proj[at, :HEAD])
        key_hat, key_inverse = normalize(proj[at, HEAD : 2 * HEAD])
        query_low, key_low = query_hat.astype(BF16), key_hat.astype(BF16)
        value_low = proj[at, 2 * HEAD : 3 * HEAD].astype(BF16)
        grad_attended = proj[at, 3 * HEAD :].astype(BF16)
        exponent = jnp.exp(dot(query_low, key_low, (1, 1)) * scaling)
        attention = exponent / jnp.sum(exponent, axis=-1, keepdims=True)
        attention_low = attention.astype(BF16)
        gproj[at, 3 * HEAD :] = dot(attention_low, value_low, (1, 0)).astype(BF16)
        gproj[at, 2 * HEAD : 3 * HEAD] = dot(attention_low, grad_attended, (0, 0)).astype(BF16)
        grad_attention = dot(grad_attended, value_low, (1, 1))
        row_total = jnp.sum(attention * grad_attention, axis=-1, keepdims=True)
        grad_scores = (attention * (grad_attention - row_total) * scaling).astype(BF16)
        grad_query_hat = dot(grad_scores, key_low, (1, 0))
        grad_key_hat = dot(grad_scores, query_low, (0, 0))
        gproj[at, :HEAD] = norm_back(grad_query_hat, query_hat, query_inverse).astype(BF16)
        gproj[at, HEAD : 2 * HEAD] = norm_back(grad_key_hat, key_hat, key_inverse).astype(BF16)


def scatter(me, mail, tok, cot, gproj, acc, sib_out, sib_in, nout, nin, fsum, fout, fin_ab, fin_c, sems):
    bs, br, ns, nr, fs, fr = sems

    def terms(yh, c):
        at = [columns((yh * 4 + i) * 2 + c) for i in range(4)]
        inner = dot(turned[: 3 * HEAD], jnp.concatenate([tok[:, a] for a in at], 1), (1, 0))
        outer = dot(turned[3 * HEAD :], jnp.concatenate([cot[:, a] for a in at], 1), (1, 0))
        return jnp.concatenate([inner, outer], 0).T.reshape(2, 2, 4, 2, 48, 4 * HEAD)

    turned = gproj[...].T
    sib = []
    for yh in range(2):
        sib_out[yh] = terms(yh, 1 - me.c).astype(BF16)
        sib.append(mail.push(sib_out.at[yh], sib_in.at[yh], bs.at[yh], br.at[yh], me.sibling()))

    def combos(stage, p):
        order = ORDERS[p][::-1]
        axis, rest, gone = order[stage], order[stage + 1:], order[:stage]
        found = []
        for n in range(2 ** len(rest)):
            found.append({a: (n >> i) & 1 for i, a in enumerate(rest)} | {a: me.low[a] for a in gone})
        return axis, found

    base = (0, 4, 6)

    def near(stage, p, half):
        axis, found = combos(stage, p)
        for n, at in enumerate(found):
            yl, xl, zl = ((1 - me.low[a]) if a == axis else at[a] for a in "yxz")
            nout[p, half, base[stage] + n] = acc[half, yl, xl, :, zl, pl.ds(16 * p, 16), :].astype(BF16)
        where = (p, half, pl.ds(base[stage], len(found)))
        k = (stage * 3 + p) * 2 + half
        return mail.push(nout.at[where], nin.at[where], ns.at[k], nr.at[k], me.step(axis, 1 - 2 * half))

    def near_add(stage, p, half):
        axis, found = combos(stage, p)
        for n, at in enumerate(found):
            yl, xl, zl = (me.low[a] if a == axis else at[a] for a in "yxz")
            place = (half, yl, xl, slice(None), zl, pl.ds(16 * p, 16), slice(None))
            acc[place] = acc[place] + nin[p, half, base[stage] + n].astype(F32)

    flight = {}
    for yh in range(2):
        acc[yh] = terms(yh, me.c)
        sib[yh].wait_recv()
        acc[yh] = acc[yh] + sib_in[yh].astype(F32)
        for p in range(3):
            flight[p, yh] = near(0, p, yh)
    for stage in range(3):
        for half in range(2):
            for p in range(3):
                flight[p, half].wait_recv()
                near_add(stage, p, half)
                if stage < 2:
                    flight[p, half] = near(stage + 1, p, half)

    for yh in range(2):
        for zf in range(4):
            block = acc[yh, me.yl, me.xl, zf, me.zl]
            for xh in range(2):
                rows = block[24 * xh : 24 * xh + 24]
                rows = jnp.concatenate([rows[:, :256], rows[:, 256:]], 0)
                fsum[yh, zf, xh] = rows
                fout[yh, zf, xh] = rows.astype(BF16)
    early, late = [], []
    for k, f in enumerate(FAR_XY):
        yh, zf, xh, to = me.far(f)
        early.append(mail.push(fout.at[yh, :, xh, EARLY], fin_ab.at[k], fs.at[k], fr.at[k], to))
    for k, f in enumerate(FAR_Z):
        yh, zf, xh, to = me.far(f)
        late.append(mail.push(fout.at[:, zf, :, LATE], fin_c.at[k], fs.at[3 + k], fr.at[3 + k], to))
    for k in range(3):
        early[k].wait_recv()
        fsum[me.yh, :, me.xh, EARLY] += fin_ab[k].astype(F32)
    fout[me.yh, :, me.xh, EARLY] = fsum[me.yh, :, me.xh, EARLY].astype(BF16)
    copies = []
    for k, f in enumerate(FAR_Z):
        yh, zf, xh, to = me.far(f)
        copies.append(
            mail.push(fout.at[me.yh, zf, me.xh, EARLY], fin_ab.at[3, k], fs.at[6 + k], fr.at[6 + k], to)
        )
    for k in range(3):
        late[k].wait_recv()
        fsum[:, me.zf, :, LATE] += fin_c[k].astype(F32)
    fout[:, me.zf, :, LATE] = fsum[:, me.zf, :, LATE].astype(BF16)
    for k, f in enumerate(FAR_XY):
        yh, zf, xh, to = me.far(f)
        copies.append(
            mail.push(fout.at[yh, me.zf, xh, LATE], fin_c.at[3, k // 2, k % 2], fs.at[9 + k], fr.at[9 + k], to)
        )
    total_ab = fsum[me.yh, me.zf, me.xh, EARLY]
    total_c = fsum[me.yh, me.zf, me.xh, LATE]
    for k in range(3):
        copies[k].wait_recv()
        total_ab = total_ab + fin_ab[3, k].astype(F32)
    for k in range(3):
        copies[3 + k].wait_recv()
        total_c = total_c + fin_c[3, k // 2, k % 2].astype(F32)
    total = jnp.concatenate([total_ab, total_c], 0)
    return jnp.concatenate([total[:24], total[24:]], 1)


def adam_step(parameter, moment_one, moment_two, gradient, decay_rate):
    fresh_one = BETA_ONE * moment_one + (1.0 - BETA_ONE) * gradient
    fresh_two = BETA_TWO * moment_two + (1.0 - BETA_TWO) * gradient * gradient
    adjusted = fresh_one / CORRECT_ONE / (jnp.sqrt(fresh_two / CORRECT_TWO) + ADAM_EPS)
    return (parameter - LEARN_RATE * (adjusted + decay_rate * parameter), fresh_one, fresh_two)


def stacked(rows):
    return jnp.concatenate([rows[:, :256], rows[:, 256:]], 0).astype(BF16)


def gain_line(place, row):
    place[...] = jnp.zeros((1, 128), F32)
    place[:, :24] = row.astype(BF16).astype(F32)


def as_row(column):
    lane = lax.broadcasted_iota(jnp.int32, (24, 24), 1)
    row = lax.broadcasted_iota(jnp.int32, (24, 24), 0)
    return jnp.sum(jnp.where(lane == row, column, 0.0), axis=0, keepdims=True)


def whole(
    tokens, cotangent, weights, first, second, gain, gain_one, gain_two,
    new_weights, new_first, new_second, new_gain, new_gain_one, new_gain_two, next_weights, next_gain,
    tok, cot, full, full_two, gfull, gnext, land, land_two, shard, gains, mean, inverse, proj, gproj,
    acc, sib_out, sib_in, nout, nin, fsum, fout, fin_ab, fin_c, small, load, rsem, *sems
):
    me = Place()
    mail = Mail()
    loads = [pltpu.make_async_copy(tokens, tok, load.at[0]), pltpu.make_async_copy(cotangent, cot, load.at[1])]
    for copy in loads:
        copy.start()
    shard[...] = stacked(weights[...])
    gain_line(gfull.at[me.yh, me.yl, me.xl, me.c, me.zf, me.zl, me.xh], gain[...])
    enter(me)

    def far_one():
        loads[0].wait()
        statistics(tok, mean, inverse, 0, 16)

    def far_two():
        statistics(tok, mean, inverse, 16, 16)

    def gains_here(shared):
        shared.wait_recv()
        gains[...] = gain_rows(gfull)
        scale_tokens(tok, gains, mean, inverse, me.c)
        loads[1].wait()

    def own_here():
        scale_tokens(tok, gains, mean, inverse, 1 - me.c)
        project(tok, cot, full, proj, me.c, True)

    nothing = lambda: None
    gather(
        me, mail, shard, full, gfull, land, sems[:8],
        (far_one, far_two, nothing, nothing, nothing, gains_here, own_here),
    )
    project(tok, cot, full, proj, 1 - me.c, False)
    attend(proj, gproj)
    gradient = scatter(
        me, mail, tok, cot, gproj, acc, sib_out, sib_in, nout, nin, fsum, fout, fin_ab, fin_c, sems[16:]
    )
    low = weights[:, : 3 * HEAD].astype(BF16).astype(F32)
    grad_gain = as_row(jnp.sum(gradient[:, : 3 * HEAD] * low, axis=1, keepdims=True))
    grad_gain = grad_gain / gain[...].astype(BF16).astype(F32)
    fresh, one, two = adam_step(weights[...], first[...], second[...], gradient, DECAY_RATE)
    saves = []
    for k, (value, to) in enumerate(((fresh, new_weights), (one, new_first), (two, new_second))):
        small[k] = value
        saves.append(pltpu.make_async_copy(small.at[k], to, load.at[2 + k]))
        saves[-1].start()
    fresh_gain, one, two = adam_step(gain[...], gain_one[...], gain_two[...], grad_gain, 0.0)
    new_gain[...], new_gain_one[...], new_gain_two[...] = fresh_gain, one, two
    shard[...] = stacked(fresh)
    gain_line(gnext.at[me.yh, me.yl, me.xl, me.c, me.zf, me.zl, me.xh], fresh_gain)

    def next_here(shared):
        shared.wait_recv()
        next_gain[...] = gain_rows(gnext)

    gather(
        me, mail, shard, full_two, gnext, land_two, sems[8:16], (nothing,) * 5 + (next_here, nothing),
        next_weights, rsem,
    )
    for copy in saves:
        copy.wait()
    mail.close()


def keep(*refs):
    count = (len(refs) - 2) // 3
    here, there, held, came, left = refs[:count], refs[count : 2 * count], refs[2 * count : 3 * count], refs[-2], refs[-1]
    pairs = []
    for i in range(count):
        if len(here[i].shape) > 2:
            for n in range(8):
                at = (n // 4, n // 2 % 2, n % 2)
                pairs.append((here[i].at[at], held[i].at[at], there[i].at[at]))
        else:
            pairs.append((here[i], held[i], there[i]))
    ins = [pltpu.make_async_copy(a, b, came.at[k]) for k, (a, b, c) in enumerate(pairs)]
    outs = [pltpu.make_async_copy(b, c, left.at[k]) for k, (a, b, c) in enumerate(pairs)]
    for copy in ins:
        copy.start()
    for a, b in zip(ins, outs):
        a.wait()
        b.start()
    for copy in outs:
        copy.wait()


def shards(
    tokens, cotangent, weights, first_moment, second_moment, norm_gain, gain_first, gain_second
):
    dma, vmem = pltpu.SemaphoreType.DMA, pltpu.VMEM
    own, line = jax.ShapeDtypeStruct((24, 512), F32), jax.ShapeDtypeStruct((1, 24), F32)
    gather_sems = [dma((12,))] * 2 + [dma((9,))] * 2 + [dma((36,))] * 2 + [dma((14,))] * 2
    out = pl.pallas_call(
        whole,
        name="whole",
        out_shape=(own,) * 3 + (line,) * 3
        + (jax.ShapeDtypeStruct(VIEW, BF16), jax.ShapeDtypeStruct((16, CHUNK), F32)),
        in_specs=[pl.BlockSpec(memory_space=pl.ANY)] * 2 + [pl.BlockSpec(memory_space=pltpu.VMEM)] * 6,
        out_specs=(pl.BlockSpec(memory_space=pl.ANY),) * 3 + (pl.BlockSpec(memory_space=pltpu.VMEM),) * 3
        + (pl.BlockSpec(memory_space=pl.ANY), pl.BlockSpec(memory_space=pltpu.VMEM)),
        scratch_shapes=[
            vmem((ROWS, 6144), BF16),
            vmem((ROWS, 6144), BF16),
            vmem(VIEW, BF16),
            vmem(VIEW, BF16),
            vmem(GVIEW, F32),
            vmem(GVIEW, F32),
            vmem((2, 4, 2, 48, 256), BF16),
            vmem((2, 4, 2, 48, 256), BF16),
            vmem((48, 256), BF16),
            vmem((16, CHUNK), F32),
            vmem((ROWS, 1), F32),
            vmem((ROWS, 1), F32),
            vmem((ROWS, 4 * HEAD), F32),
            vmem((ROWS, 4 * HEAD), BF16),
            vmem((2, 2, 2, 4, 2, 48, 512), F32),
            vmem((2, 2, 2, 4, 2, 48, 512), BF16),
            vmem((2, 2, 2, 4, 2, 48, 512), BF16),
            vmem((3, 2, 7, 4, 16, 512), BF16),
            vmem((3, 2, 7, 4, 16, 512), BF16),
            vmem((2, 4, 2, 48, 256), F32),
            vmem((2, 4, 2, 48, 256), BF16),
            vmem((4, 4, 32, 256), BF16),
            vmem((4, 2, 2, 16, 256), BF16),
            vmem((3, 24, 512), F32),
            dma((5,)),
            dma((14,)),
        ] + gather_sems * 2 + [dma((2,))] * 2 + [dma((18,))] * 2 + [dma((12,))] * 2,
        compiler_params=pltpu.CompilerParams(
            collective_id=1, has_side_effects=True, vmem_limit_bytes=56 << 20
        ),
    )(
        tokens, cotangent, weights, first_moment, second_moment,
        norm_gain.reshape(1, 24), gain_first.reshape(1, 24), gain_second.reshape(1, 24),
    )
    kept = (0, 1, 2, 3, 4, 5, 6)
    copies = pl.pallas_call(
        keep,
        name="keep",
        out_shape=tuple(jax.ShapeDtypeStruct(out[i].shape, out[i].dtype) for i in kept),
        in_specs=[pl.BlockSpec(memory_space=pl.ANY)] * len(kept),
        out_specs=(pl.BlockSpec(memory_space=pl.ANY),) * len(kept),
        scratch_shapes=[vmem(out[i].shape, out[i].dtype) for i in kept] + [dma((len(kept) + 7,))] * 2,
        compiler_params=pltpu.CompilerParams(vmem_limit_bytes=16 << 20),
    )(*(out[i] for i in kept))
    return (
        *copies[:3],
        *(copy.reshape(24) for copy in copies[3:6]),
        copies[6].reshape(6144, 512),
        out[7].reshape(6144).astype(BF16),
    )


def solution(mesh):
    rows, line = P(("gx", "gy"), None), P(("gx", "gy"))
    return jax.shard_map(
        shards,
        mesh=mesh,
        in_specs=(rows,) * 5 + (line,) * 3,
        out_specs=(rows,) * 3 + (line,) * 3 + (P(), P()),
        check_vma=False,
    )
```

```python
import functools

import jax
import jax.numpy as jnp
from jax import lax
from jax.experimental import pallas as pl
from jax.experimental.pallas import tpu as pltpu
from jax.sharding import PartitionSpec as P

IMG_TOK = 256
EPS_NORM = 1e-06
BETA_ONE = 0.9
BETA_TWO = 0.95
LEARN_RATE = 0.001
DECAY_RATE = 0.1
ADAM_EPS = 1e-08
CORRECT_ONE = 1.0 - 0.9**10
CORRECT_TWO = 1.0 - 0.95**10
MESH = pl.DeviceIdType.MESH
BF16, F32 = jnp.bfloat16, jnp.float32

VIEW = (2, 2, 2, 2, 4, 2, 48, 512)
GVIEW = (2, 2, 2, 2, 4, 2, 2, 1, 128)
ROWS, HEAD, CHUNK = 512, 128, 384
FAR_Z = [(0, dz, 0) for dz in (1, 3, 2)]
FAR_XY = [(0, 0, 1), (1, 0, 0), (1, 0, 1)]
EARLY, LATE = pl.ds(0, 32), pl.ds(32, 16)
ORDERS = (("z", "y", "x"), ("x", "z", "y"), ("y", "x", "z"))


class Place:
    def __init__(self):
        gx, gy = lax.axis_index("gx"), lax.axis_index("gy")
        self.y, self.z = gx // 4, gy // 2
        self.xl, self.c, self.xh = lax.rem(gx // 2, 2), lax.rem(gx, 2), lax.rem(gy, 2)
        self.yh, self.yl, self.zf, self.zl = self.y // 2, lax.rem(self.y, 2), self.z // 2, lax.rem(self.z, 2)
        self.x = self.xh * 2 + self.xl
        self.low = {"x": self.xl, "y": self.yl, "z": self.zl}

    def device(self, x, y, z, c):
        return (y * 4 + lax.rem(x, 2) * 2 + c, z * 2 + x // 2)

    def step(self, axis, by):
        x, y, z = self.x, self.y, self.z
        if axis == "x":
            x = lax.rem(x + by + 4, 4)
        elif axis == "y":
            y = lax.rem(y + by + 4, 4)
        else:
            z = lax.rem(z + by + 8, 8)
        return self.device(x, y, z, self.c)

    def sibling(self):
        return self.device(self.x, self.y, self.z, 1 - self.c)

    def far(self, offset):
        dy, dz, dx = offset
        yh, zf, xh = lax.rem(self.yh + dy, 2), lax.rem(self.zf + dz, 4), lax.rem(self.xh + dx, 2)
        return yh, zf, xh, self.device(xh * 2 + self.xl, yh * 2 + self.yl, zf * 2 + self.zl, self.c)


def enter(me):
    barrier = pltpu.get_barrier_semaphore()
    others = [me.far(f)[3] for f in FAR_Z + FAR_XY] + [me.step(a, b) for a in "xyz" for b in (1, -1)] + [me.sibling()]
    for other in others:
        pl.semaphore_signal(barrier, inc=1, device_id=other, device_id_type=MESH)
    pl.semaphore_wait(barrier, len(others))


class Mail:
    def __init__(self):
        self.sends = []

    def push(self, src, dst, ssem, rsem, to):
        copy = pltpu.make_async_remote_copy(src, dst, ssem, rsem, device_id=to, device_id_type=MESH)
        copy.start()
        self.sends.append(copy)
        return copy

    def close(self):
        for copy in self.sends:
            copy.wait_send()


def gather(me, mail, shard, full, gfull, land, sems, between, result=None, rsem=None):
    fs, fr, gs, gr, ns, nr, ss, sr = sems
    yh, zf, xh = me.yh, me.zf, me.xh
    land[yh, zf, xh] = shard[...]

    def far(first, src_z, src_xy):
        copies = []
        for group, src in ((FAR_Z, src_z), (FAR_XY, src_xy)):
            for f in group:
                k = first + len(copies)
                copies.append(mail.push(src, src, fs.at[k], fr.at[k], me.far(f)[3]))
        return copies

    def far_gain(first, group, src):
        return [
            mail.push(src, src, gs.at[first + k], gr.at[first + k], me.far(f)[3]) for k, f in enumerate(group)
        ]

    own_gain = gfull.at[:, me.yl, me.xl, me.c, :, me.zl]
    gains = far_gain(0, FAR_Z, own_gain.at[yh, zf, xh])
    copies = far(0, land.at[yh, zf, xh, EARLY], land.at[yh, zf, xh, LATE])
    between[0]()
    for copy in gains:
        copy.wait_recv()
    gains = far_gain(3, FAR_XY, own_gain.at[yh, :, xh])
    for copy in copies:
        copy.wait_recv()
    copies = far(6, land.at[:, zf, :, LATE], land.at[yh, :, xh, EARLY])
    between[1]()
    for copy in gains + copies:
        copy.wait_recv()

    def near_gain(stage):
        axis, done = "zyx"[stage], "zyx"[:stage]
        at = {a: (slice(None) if a in done else me.low[a]) for a in "xyz"}
        src = gfull.at[:, at["y"], at["x"], me.c, :, at["z"]]
        return mail.push(src, src, gs.at[6 + stage], gr.at[6 + stage], me.step(axis, 1))

    gflight = near_gain(0)
    for h in range(2):
        for f in range(4):
            a, b = (land[h, f, g].astype(F32) for g in range(2))
            block = jnp.concatenate(
                [jnp.concatenate([a[:24], b[:24]], 0), jnp.concatenate([a[24:], b[24:]], 0)], 1
            )
            full[h, me.yl, me.xl, me.c, f, me.zl] = block.astype(BF16)

    def part(ref, done, half, zfar, p, fresh=None):
        at = {a: (slice(None) if a in done else me.low[a]) for a in "xyz"}
        if fresh is not None:
            at[fresh] = 1 - me.low[fresh]
        return ref.at[half, at["y"], at["x"], me.c, zfar, at["z"], pl.ds(16 * p, 16)]

    shared, local = [], []

    def share(view, src):
        k = len(shared)
        to = src if result is None else result
        shared.append(mail.push(view(src), view(to), ss.at[k], sr.at[k], me.sibling()))
        if result is not None:
            local.append(pltpu.make_async_copy(view(src), view(result), rsem.at[k]))
            local[-1].start()

    both = slice(None)
    flight = {}

    def near(stage, q):
        for p in range(3):
            axis, done = ORDERS[p][stage], ORDERS[p][:stage]
            for half in range(2):
                if stage > 0:
                    flight[stage - 1, p, half, q].wait_recv()
                src = part(full, done, half, pl.ds(2 * q, 2), p)
                k = ((stage * 3 + p) * 2 + half) * 2 + q
                flight[stage, p, half, q] = mail.push(src, src, ns.at[k], nr.at[k], me.step(axis, 1 - 2 * half))

    def spread_news(stage, zfar):
        for p in range(3):
            share(lambda ref: part(ref, ORDERS[p][:stage], both, zfar, p, ORDERS[p][stage]), full)

    near(0, 0)
    near(0, 1)
    share(lambda ref: ref.at[:, me.yl, me.xl, me.c, :, me.zl], full)
    between[2]()
    for stage in (1, 2):
        gflight.wait_recv()
        gflight = near_gain(stage)
        near(stage, 0)
        near(stage, 1)
        spread_news(stage - 1, both)
        between[2 + stage]()
    gflight.wait_recv()
    place = gfull.at[:, :, :, me.c]
    shared.append(mail.push(place, place, ss.at[7], sr.at[7], me.sibling()))
    between[5](shared[-1])
    for q in range(2):
        for p in range(3):
            for half in range(2):
                flight[2, p, half, q].wait_recv()
        spread_news(2, pl.ds(2 * q, 2))
        between[6 + q]()
    for k, copy in enumerate(shared):
        if k != 7:
            copy.wait_recv()
    for copy in local:
        copy.wait()


def gain_rows(gfull):
    feature = lax.broadcasted_iota(jnp.int32, (128, CHUNK), 1).astype(F32)
    lane = lax.broadcasted_iota(jnp.int32, (128, CHUNK), 0).astype(F32)
    spread = jnp.where(feature - 24.0 * jnp.floor((feature + 0.5) * (1.0 / 24.0)) == lane, 1.0, 0.0).astype(BF16)
    feature = lax.broadcasted_iota(jnp.int32, (16, CHUNK), 1)
    source = lax.broadcasted_iota(jnp.int32, (16, CHUNK), 0)
    pick = jnp.where((feature >= 24 * source) & (feature < 24 * source + 24), 1.0, 0.0)
    flat = gfull[...].reshape(256, 128).astype(BF16)
    wide = jnp.dot(flat, spread, preferred_element_type=F32)
    return jnp.sum(wide.reshape(16, 16, CHUNK) * pick[None], axis=1)


def columns(j):
    return pl.ds(pl.multiple_of(j * CHUNK, 128), CHUNK)


def statistics(tok, mean, inverse, first, count):
    def rows(i, carry):
        at = pl.ds(pl.multiple_of(i * 16, 16), 16)
        values = tok[at, :].astype(F32)
        average = jnp.mean(values, axis=-1, keepdims=True)
        centred = values - average
        spread = jnp.mean(centred * centred, axis=-1, keepdims=True)
        mean[at, :] = average
        inverse[at, :] = lax.rsqrt(spread + EPS_NORM)
        return carry

    lax.fori_loop(first, first + count, rows, 0)


def scale_tokens(tok, gains, mean, inverse, c):
    def chunk(i, carry):
        j = i * 2 + c
        at = columns(j)
        standard = (tok[:, at].astype(F32) - mean[...]) * inverse[...]
        tok[:, at] = (standard * gains[pl.ds(j, 1), :]).astype(BF16)
        return carry

    lax.fori_loop(0, 8, chunk, 0)


def project(tok, cot, full, proj, c, first):
    at = [columns(i * 2 + c) for i in range(8)]
    low = full[:, :, :, c].reshape(8 * CHUNK, 4 * HEAD)
    inner = jnp.dot(jnp.concatenate([tok[:, a] for a in at], 1), low[:, : 3 * HEAD], preferred_element_type=F32)
    outer = jnp.dot(jnp.concatenate([cot[:, a] for a in at], 1), low[:, 3 * HEAD :], preferred_element_type=F32)
    if not first:
        inner, outer = inner + proj[:, : 3 * HEAD], outer + proj[:, 3 * HEAD :]
    proj[:, : 3 * HEAD] = inner
    proj[:, 3 * HEAD :] = outer


def normalize(values):
    average = jnp.mean(values, axis=-1, keepdims=True)
    centred = values - average
    inverse = lax.rsqrt(jnp.mean(centred * centred, axis=-1, keepdims=True) + EPS_NORM)
    return (centred * inverse, inverse)


def norm_back(grad_hat, normed, inverse):
    first_part = jnp.mean(grad_hat, axis=-1, keepdims=True)
    second_part = normed * jnp.mean(grad_hat * normed, axis=-1, keepdims=True)
    return inverse * (grad_hat - first_part - second_part)


def dot(left, right, dims):
    return lax.dot_general(left, right, (((dims[0],), (dims[1],)), ((), ())), preferred_element_type=F32)


def attend(proj, gproj):
    scaling = HEAD ** (-0.5)
    for image in range(ROWS // IMG_TOK):
        at = pl.ds(image * IMG_TOK, IMG_TOK)
        query_hat, query_inverse = normalize(proj[at, :HEAD])
        key_hat, key_inverse = normalize(proj[at, HEAD : 2 * HEAD])
        query_low, key_low = query_hat.astype(BF16), key_hat.astype(BF16)
        value_low = proj[at, 2 * HEAD : 3 * HEAD].astype(BF16)
        grad_attended = proj[at, 3 * HEAD :].astype(BF16)
        exponent = jnp.exp(dot(query_low, key_low, (1, 1)) * scaling)
        attention = exponent / jnp.sum(exponent, axis=-1, keepdims=True)
        attention_low = attention.astype(BF16)
        gproj[at, 3 * HEAD :] = dot(attention_low, value_low, (1, 0)).astype(BF16)
        gproj[at, 2 * HEAD : 3 * HEAD] = dot(attention_low, grad_attended, (0, 0)).astype(BF16)
        grad_attention = dot(grad_attended, value_low, (1, 1))
        row_total = jnp.sum(attention * grad_attention, axis=-1, keepdims=True)
        grad_scores = (attention * (grad_attention - row_total) * scaling).astype(BF16)
        grad_query_hat = dot(grad_scores, key_low, (1, 0))
        grad_key_hat = dot(grad_scores, query_low, (0, 0))
        gproj[at, :HEAD] = norm_back(grad_query_hat, query_hat, query_inverse).astype(BF16)
        gproj[at, HEAD : 2 * HEAD] = norm_back(grad_key_hat, key_hat, key_inverse).astype(BF16)


def scatter(me, mail, tok, cot, gproj, acc, sib_out, sib_in, nout, nin, fsum, fout, fin_ab, fin_c, sems):
    bs, br, ns, nr, fs, fr = sems

    def terms(yh, c):
        at = [columns((yh * 4 + i) * 2 + c) for i in range(4)]
        inner = dot(turned[: 3 * HEAD], jnp.concatenate([tok[:, a] for a in at], 1), (1, 0))
        outer = dot(turned[3 * HEAD :], jnp.concatenate([cot[:, a] for a in at], 1), (1, 0))
        return jnp.concatenate([inner, outer], 0).T.reshape(2, 2, 4, 2, 48, 4 * HEAD)

    turned = gproj[...].T
    sib = []
    for yh in range(2):
        sib_out[yh] = terms(yh, 1 - me.c).astype(BF16)
        sib.append(mail.push(sib_out.at[yh], sib_in.at[yh], bs.at[yh], br.at[yh], me.sibling()))

    def combos(stage, p):
        order = ORDERS[p][::-1]
        axis, rest, gone = order[stage], order[stage + 1:], order[:stage]
        found = []
        for n in range(2 ** len(rest)):
            found.append({a: (n >> i) & 1 for i, a in enumerate(rest)} | {a: me.low[a] for a in gone})
        return axis, found

    base = (0, 4, 6)

    def near(stage, p, yh, way):
        axis, found = combos(stage, p)
        zfar = pl.ds(2 * way, 2)
        for n, at in enumerate(found):
            yl, xl, zl = ((1 - me.low[a]) if a == axis else at[a] for a in "yxz")
            nout[p, yh, base[stage] + n, zfar] = acc[yh, yl, xl, zfar, zl, pl.ds(16 * p, 16), :].astype(BF16)
        where = (p, yh, pl.ds(base[stage], len(found)), zfar)
        k = ((stage * 3 + p) * 2 + yh) * 2 + way
        return mail.push(nout.at[where], nin.at[where], ns.at[k], nr.at[k], me.step(axis, 1 - 2 * way))

    def near_add(stage, p, yh, way):
        axis, found = combos(stage, p)
        zfar = pl.ds(2 * way, 2)
        for n, at in enumerate(found):
            yl, xl, zl = (me.low[a] if a == axis else at[a] for a in "yxz")
            place = (yh, yl, xl, zfar, zl, pl.ds(16 * p, 16), slice(None))
            acc[place] = acc[place] + nin[p, yh, base[stage] + n, zfar].astype(F32)

    flight = {}
    for yh in range(2):
        acc[yh] = terms(yh, me.c)
        sib[yh].wait_recv()
        acc[yh] = acc[yh] + sib_in[yh].astype(F32)
        for p in range(3):
            for way in range(2):
                flight[p, yh, way] = near(0, p, yh, way)
    for stage in range(3):
        for yh in range(2):
            for p in range(3):
                for way in range(2):
                    flight[p, yh, way].wait_recv()
                    near_add(stage, p, yh, way)
                    if stage < 2:
                        flight[p, yh, way] = near(stage + 1, p, yh, way)

    for yh in range(2):
        for zf in range(4):
            block = acc[yh, me.yl, me.xl, zf, me.zl]
            for xh in range(2):
                rows = block[24 * xh : 24 * xh + 24]
                rows = jnp.concatenate([rows[:, :256], rows[:, 256:]], 0)
                fsum[yh, zf, xh] = rows
                fout[yh, zf, xh] = rows.astype(BF16)
    early, late = [], []
    for k, f in enumerate(FAR_XY):
        yh, zf, xh, to = me.far(f)
        early.append(mail.push(fout.at[yh, :, xh, EARLY], fin_ab.at[k], fs.at[k], fr.at[k], to))
    for k, f in enumerate(FAR_Z):
        yh, zf, xh, to = me.far(f)
        late.append(mail.push(fout.at[:, zf, :, LATE], fin_c.at[k], fs.at[3 + k], fr.at[3 + k], to))
    for k in range(3):
        early[k].wait_recv()
        fsum[me.yh, :, me.xh, EARLY] += fin_ab[k].astype(F32)
    fout[me.yh, :, me.xh, EARLY] = fsum[me.yh, :, me.xh, EARLY].astype(BF16)
    copies = []
    for k, f in enumerate(FAR_Z):
        yh, zf, xh, to = me.far(f)
        copies.append(
            mail.push(fout.at[me.yh, zf, me.xh, EARLY], fin_ab.at[3, k], fs.at[6 + k], fr.at[6 + k], to)
        )
    for k in range(3):
        late[k].wait_recv()
        fsum[:, me.zf, :, LATE] += fin_c[k].astype(F32)
    fout[:, me.zf, :, LATE] = fsum[:, me.zf, :, LATE].astype(BF16)
    for k, f in enumerate(FAR_XY):
        yh, zf, xh, to = me.far(f)
        copies.append(
            mail.push(fout.at[yh, me.zf, xh, LATE], fin_c.at[3, k // 2, k % 2], fs.at[9 + k], fr.at[9 + k], to)
        )
    total_ab = fsum[me.yh, me.zf, me.xh, EARLY]
    total_c = fsum[me.yh, me.zf, me.xh, LATE]
    for k in range(3):
        copies[k].wait_recv()
        total_ab = total_ab + fin_ab[3, k].astype(F32)
    for k in range(3):
        copies[3 + k].wait_recv()
        total_c = total_c + fin_c[3, k // 2, k % 2].astype(F32)
    total = jnp.concatenate([total_ab, total_c], 0)
    return jnp.concatenate([total[:24], total[24:]], 1)


def adam_step(parameter, moment_one, moment_two, gradient, decay_rate):
    fresh_one = BETA_ONE * moment_one + (1.0 - BETA_ONE) * gradient
    fresh_two = BETA_TWO * moment_two + (1.0 - BETA_TWO) * gradient * gradient
    adjusted = fresh_one / CORRECT_ONE / (jnp.sqrt(fresh_two / CORRECT_TWO) + ADAM_EPS)
    return (parameter - LEARN_RATE * (adjusted + decay_rate * parameter), fresh_one, fresh_two)


def stacked(rows):
    return jnp.concatenate([rows[:, :256], rows[:, 256:]], 0).astype(BF16)


def gain_line(place, row):
    place[...] = jnp.zeros((1, 128), F32)
    place[:, :24] = row.astype(BF16).astype(F32)


def as_row(column):
    lane = lax.broadcasted_iota(jnp.int32, (24, 24), 1)
    row = lax.broadcasted_iota(jnp.int32, (24, 24), 0)
    return jnp.sum(jnp.where(lane == row, column, 0.0), axis=0, keepdims=True)


def whole(
    tokens, cotangent, weights, first, second, gain, gain_one, gain_two,
    new_weights, new_first, new_second, new_gain, new_gain_one, new_gain_two, next_weights, next_gain,
    tok, cot, full, full_two, gfull, gnext, land, land_two, shard, gains, mean, inverse, proj, gproj,
    acc, sib_out, sib_in, nout, nin, fsum, fout, fin_ab, fin_c, small, load, rsem, *sems
):
    me = Place()
    mail = Mail()
    loads = [pltpu.make_async_copy(tokens, tok, load.at[0]), pltpu.make_async_copy(cotangent, cot, load.at[1])]
    for copy in loads:
        copy.start()
    shard[...] = stacked(weights[...])
    gain_line(gfull.at[me.yh, me.yl, me.xl, me.c, me.zf, me.zl, me.xh], gain[...])
    enter(me)

    def far_one():
        loads[0].wait()
        statistics(tok, mean, inverse, 0, 14)

    def far_two():
        statistics(tok, mean, inverse, 14, 10)

    def near_one():
        statistics(tok, mean, inverse, 24, 8)

    def gains_here(shared):
        shared.wait_recv()
        gains[...] = gain_rows(gfull)
        scale_tokens(tok, gains, mean, inverse, me.c)
        loads[1].wait()

    def scale_here():
        scale_tokens(tok, gains, mean, inverse, 1 - me.c)

    def own_here():
        project(tok, cot, full, proj, me.c, True)

    nothing = lambda: None
    gather(
        me, mail, shard, full, gfull, land, sems[:8],
        (far_one, far_two, near_one, nothing, nothing, gains_here, scale_here, own_here),
    )
    project(tok, cot, full, proj, 1 - me.c, False)
    attend(proj, gproj)
    gradient = scatter(
        me, mail, tok, cot, gproj, acc, sib_out, sib_in, nout, nin, fsum, fout, fin_ab, fin_c, sems[16:]
    )
    low = weights[:, : 3 * HEAD].astype(BF16).astype(F32)
    grad_gain = as_row(jnp.sum(gradient[:, : 3 * HEAD] * low, axis=1, keepdims=True))
    grad_gain = grad_gain / gain[...].astype(BF16).astype(F32)
    fresh, one, two = adam_step(weights[...], first[...], second[...], gradient, DECAY_RATE)
    saves = []
    for k, (value, to) in enumerate(((fresh, new_weights), (one, new_first), (two, new_second))):
        small[k] = value
        saves.append(pltpu.make_async_copy(small.at[k], to, load.at[2 + k]))
        saves[-1].start()
    fresh_gain, one, two = adam_step(gain[...], gain_one[...], gain_two[...], grad_gain, 0.0)
    new_gain[...], new_gain_one[...], new_gain_two[...] = fresh_gain, one, two
    shard[...] = stacked(fresh)
    gain_line(gnext.at[me.yh, me.yl, me.xl, me.c, me.zf, me.zl, me.xh], fresh_gain)

    def next_here(shared):
        shared.wait_recv()
        next_gain[...] = gain_rows(gnext)

    gather(
        me, mail, shard, full_two, gnext, land_two, sems[8:16], (nothing,) * 5 + (next_here, nothing, nothing),
        next_weights, rsem,
    )
    for copy in saves:
        copy.wait()
    mail.close()


def keep(*refs):
    count = (len(refs) - 2) // 3
    here, there, held, came, left = refs[:count], refs[count : 2 * count], refs[2 * count : 3 * count], refs[-2], refs[-1]
    pairs = []
    for i in range(count):
        if len(here[i].shape) > 2:
            for n in range(8):
                at = (n // 4, n // 2 % 2, n % 2)
                pairs.append((here[i].at[at], held[i].at[at], there[i].at[at]))
        else:
            pairs.append((here[i], held[i], there[i]))
    ins = [pltpu.make_async_copy(a, b, came.at[k]) for k, (a, b, c) in enumerate(pairs)]
    outs = [pltpu.make_async_copy(b, c, left.at[k]) for k, (a, b, c) in enumerate(pairs)]
    for copy in ins:
        copy.start()
    for a, b in zip(ins, outs):
        a.wait()
        b.start()
    for copy in outs:
        copy.wait()


def shards(
    tokens, cotangent, weights, first_moment, second_moment, norm_gain, gain_first, gain_second
):
    dma, vmem = pltpu.SemaphoreType.DMA, pltpu.VMEM
    own, line = jax.ShapeDtypeStruct((24, 512), F32), jax.ShapeDtypeStruct((1, 24), F32)
    gather_sems = [dma((12,))] * 2 + [dma((9,))] * 2 + [dma((36,))] * 2 + [dma((14,))] * 2
    out = pl.pallas_call(
        whole,
        name="whole",
        out_shape=(own,) * 3 + (line,) * 3
        + (jax.ShapeDtypeStruct(VIEW, BF16), jax.ShapeDtypeStruct((16, CHUNK), F32)),
        in_specs=[pl.BlockSpec(memory_space=pl.ANY)] * 2 + [pl.BlockSpec(memory_space=pltpu.VMEM)] * 6,
        out_specs=(pl.BlockSpec(memory_space=pl.ANY),) * 3 + (pl.BlockSpec(memory_space=pltpu.VMEM),) * 3
        + (pl.BlockSpec(memory_space=pl.ANY), pl.BlockSpec(memory_space=pltpu.VMEM)),
        scratch_shapes=[
            vmem((ROWS, 6144), BF16),
            vmem((ROWS, 6144), BF16),
            vmem(VIEW, BF16),
            vmem(VIEW, BF16),
            vmem(GVIEW, F32),
            vmem(GVIEW, F32),
            vmem((2, 4, 2, 48, 256), BF16),
            vmem((2, 4, 2, 48, 256), BF16),
            vmem((48, 256), BF16),
            vmem((16, CHUNK), F32),
            vmem((ROWS, 1), F32),
            vmem((ROWS, 1), F32),
            vmem((ROWS, 4 * HEAD), F32),
            vmem((ROWS, 4 * HEAD), BF16),
            vmem((2, 2, 2, 4, 2, 48, 512), F32),
            vmem((2, 2, 2, 4, 2, 48, 512), BF16),
            vmem((2, 2, 2, 4, 2, 48, 512), BF16),
            vmem((3, 2, 7, 4, 16, 512), BF16),
            vmem((3, 2, 7, 4, 16, 512), BF16),
            vmem((2, 4, 2, 48, 256), F32),
            vmem((2, 4, 2, 48, 256), BF16),
            vmem((4, 4, 32, 256), BF16),
            vmem((4, 2, 2, 16, 256), BF16),
            vmem((3, 24, 512), F32),
            dma((5,)),
            dma((14,)),
        ] + gather_sems * 2 + [dma((2,))] * 2 + [dma((36,))] * 2 + [dma((12,))] * 2,
        compiler_params=pltpu.CompilerParams(
            collective_id=1, has_side_effects=True, vmem_limit_bytes=56 << 20
        ),
    )(
        tokens, cotangent, weights, first_moment, second_moment,
        norm_gain.reshape(1, 24), gain_first.reshape(1, 24), gain_second.reshape(1, 24),
    )
    kept = (0, 1, 2, 3, 4, 5, 6)
    copies = pl.pallas_call(
        keep,
        name="keep",
        out_shape=tuple(jax.ShapeDtypeStruct(out[i].shape, out[i].dtype) for i in kept),
        in_specs=[pl.BlockSpec(memory_space=pltpu.HBM)] * len(kept),
        out_specs=(pl.BlockSpec(memory_space=pl.ANY),) * len(kept),
        scratch_shapes=[vmem(out[i].shape, out[i].dtype) for i in kept] + [dma((len(kept) + 7,))] * 2,
        compiler_params=pltpu.CompilerParams(vmem_limit_bytes=16 << 20),
    )(*(out[i] for i in kept))
    return (
        *copies[:3],
        *(copy.reshape(24) for copy in copies[3:6]),
        copies[6].reshape(6144, 512),
        out[7].reshape(6144).astype(BF16),
    )


def solution(mesh):
    rows, line = P(("gx", "gy"), None), P(("gx", "gy"))
    return jax.shard_map(
        shards,
        mesh=mesh,
        in_specs=(rows,) * 5 + (line,) * 3,
        out_specs=(rows,) * 3 + (line,) * 3 + (P(), P()),
        check_vma=False,
    )
```

```python
import functools

import jax
import jax.numpy as jnp
from jax import lax
from jax.experimental import pallas as pl
from jax.experimental.pallas import tpu as pltpu
from jax.sharding import PartitionSpec as P

IMG_TOK = 256
EPS_NORM = 1e-06
BETA_ONE = 0.9
BETA_TWO = 0.95
LEARN_RATE = 0.001
DECAY_RATE = 0.1
ADAM_EPS = 1e-08
CORRECT_ONE = 1.0 - 0.9**10
CORRECT_TWO = 1.0 - 0.95**10
MESH = pl.DeviceIdType.MESH
BF16, F32 = jnp.bfloat16, jnp.float32

VIEW = (2, 2, 2, 2, 4, 2, 48, 512)
GVIEW = (2, 2, 2, 2, 4, 2, 2, 1, 128)
ROWS, HEAD, CHUNK = 512, 128, 384
FAR_Z = [(0, dz, 0) for dz in (1, 3, 2)]
FAR_XY = [(0, 0, 1), (1, 0, 0), (1, 0, 1)]
EARLY, LATE = pl.ds(0, 32), pl.ds(32, 16)
ORDERS = (("z", "y", "x"), ("x", "z", "y"), ("y", "x", "z"))


class Place:
    def __init__(self):
        gx, gy = lax.axis_index("gx"), lax.axis_index("gy")
        self.y, self.z = gx // 4, gy // 2
        self.xl, self.c, self.xh = lax.rem(gx // 2, 2), lax.rem(gx, 2), lax.rem(gy, 2)
        self.yh, self.yl, self.zf, self.zl = self.y // 2, lax.rem(self.y, 2), self.z // 2, lax.rem(self.z, 2)
        self.x = self.xh * 2 + self.xl
        self.low = {"x": self.xl, "y": self.yl, "z": self.zl}

    def device(self, x, y, z, c):
        return (y * 4 + lax.rem(x, 2) * 2 + c, z * 2 + x // 2)

    def step(self, axis, by):
        x, y, z = self.x, self.y, self.z
        if axis == "x":
            x = lax.rem(x + by + 4, 4)
        elif axis == "y":
            y = lax.rem(y + by + 4, 4)
        else:
            z = lax.rem(z + by + 8, 8)
        return self.device(x, y, z, self.c)

    def sibling(self):
        return self.device(self.x, self.y, self.z, 1 - self.c)

    def far(self, offset):
        dy, dz, dx = offset
        yh, zf, xh = lax.rem(self.yh + dy, 2), lax.rem(self.zf + dz, 4), lax.rem(self.xh + dx, 2)
        return yh, zf, xh, self.device(xh * 2 + self.xl, yh * 2 + self.yl, zf * 2 + self.zl, self.c)


def enter(me):
    barrier = pltpu.get_barrier_semaphore()
    others = [me.far(f)[3] for f in FAR_Z + FAR_XY] + [me.step(a, b) for a in "xyz" for b in (1, -1)] + [me.sibling()]
    for other in others:
        pl.semaphore_signal(barrier, inc=1, device_id=other, device_id_type=MESH)
    pl.semaphore_wait(barrier, len(others))


class Mail:
    def __init__(self):
        self.sends = []

    def push(self, src, dst, ssem, rsem, to):
        copy = pltpu.make_async_remote_copy(src, dst, ssem, rsem, device_id=to, device_id_type=MESH)
        copy.start()
        self.sends.append(copy)
        return copy

    def close(self):
        for copy in self.sends:
            copy.wait_send()


def gather(me, mail, shard, full, gfull, land, sems, between, result=None, rsem=None):
    fs, fr, gs, gr, ns, nr, ss, sr = sems
    yh, zf, xh = me.yh, me.zf, me.xh
    land[yh, zf, xh] = shard[...]

    def far(first, src_z, src_xy):
        copies = []
        for group, src in ((FAR_Z, src_z), (FAR_XY, src_xy)):
            for f in group:
                k = first + len(copies)
                copies.append(mail.push(src, src, fs.at[k], fr.at[k], me.far(f)[3]))
        return copies

    def far_gain(first, group, src):
        return [
            mail.push(src, src, gs.at[first + k], gr.at[first + k], me.far(f)[3]) for k, f in enumerate(group)
        ]

    own_gain = gfull.at[:, me.yl, me.xl, me.c, :, me.zl]
    gains = far_gain(0, FAR_Z, own_gain.at[yh, zf, xh])
    copies = far(0, land.at[yh, zf, xh, EARLY], land.at[yh, zf, xh, LATE])
    between[0]()
    for copy in gains:
        copy.wait_recv()
    gains = far_gain(3, FAR_XY, own_gain.at[yh, :, xh])
    for copy in copies:
        copy.wait_recv()
    copies = far(6, land.at[:, zf, :, LATE], land.at[yh, :, xh, EARLY])
    between[1]()
    for copy in gains + copies:
        copy.wait_recv()

    def near_gain(stage):
        axis, done = "zyx"[stage], "zyx"[:stage]
        at = {a: (slice(None) if a in done else me.low[a]) for a in "xyz"}
        src = gfull.at[:, at["y"], at["x"], me.c, :, at["z"]]
        return mail.push(src, src, gs.at[6 + stage], gr.at[6 + stage], me.step(axis, 1))

    gflight = near_gain(0)
    for h in range(2):
        for f in range(4):
            a, b = (land[h, f, g].astype(F32) for g in range(2))
            block = jnp.concatenate(
                [jnp.concatenate([a[:24], b[:24]], 0), jnp.concatenate([a[24:], b[24:]], 0)], 1
            )
            full[h, me.yl, me.xl, me.c, f, me.zl] = block.astype(BF16)

    def part(ref, done, half, zfar, p, fresh=None):
        at = {a: (slice(None) if a in done else me.low[a]) for a in "xyz"}
        if fresh is not None:
            at[fresh] = 1 - me.low[fresh]
        return ref.at[half, at["y"], at["x"], me.c, zfar, at["z"], pl.ds(16 * p, 16)]

    shared, local = [], []

    def share(view, src):
        k = len(shared)
        to = src if result is None else result
        shared.append(mail.push(view(src), view(to), ss.at[k], sr.at[k], me.sibling()))
        if result is not None:
            local.append(pltpu.make_async_copy(view(src), view(result), rsem.at[k]))
            local[-1].start()

    both = slice(None)
    flight = {}

    def near(stage, q):
        for p in range(3):
            axis, done = ORDERS[p][stage], ORDERS[p][:stage]
            for half in range(2):
                if stage > 0:
                    flight[stage - 1, p, half, q].wait_recv()
                src = part(full, done, half, pl.ds(2 * q, 2), p)
                k = ((stage * 3 + p) * 2 + half) * 2 + q
                flight[stage, p, half, q] = mail.push(src, src, ns.at[k], nr.at[k], me.step(axis, 1 - 2 * half))

    def spread_news(stage, zfar):
        for p in range(3):
            share(lambda ref: part(ref, ORDERS[p][:stage], both, zfar, p, ORDERS[p][stage]), full)

    near(0, 0)
    near(0, 1)
    share(lambda ref: ref.at[:, me.yl, me.xl, me.c, :, me.zl], full)
    between[2]()
    for stage in (1, 2):
        gflight.wait_recv()
        gflight = near_gain(stage)
        near(stage, 0)
        near(stage, 1)
        spread_news(stage - 1, both)
        between[2 + stage]()
    gflight.wait_recv()
    place = gfull.at[:, :, :, me.c]
    shared.append(mail.push(place, place, ss.at[7], sr.at[7], me.sibling()))
    between[5](shared[-1])
    for q in range(2):
        for p in range(3):
            for half in range(2):
                flight[2, p, half, q].wait_recv()
        spread_news(2, pl.ds(2 * q, 2))
        between[6 + q]()
    for k, copy in enumerate(shared):
        if k != 7:
            copy.wait_recv()
    for copy in local:
        copy.wait()


def gain_rows(gfull):
    feature = lax.broadcasted_iota(jnp.int32, (128, CHUNK), 1).astype(F32)
    lane = lax.broadcasted_iota(jnp.int32, (128, CHUNK), 0).astype(F32)
    spread = jnp.where(feature - 24.0 * jnp.floor((feature + 0.5) * (1.0 / 24.0)) == lane, 1.0, 0.0).astype(BF16)
    feature = lax.broadcasted_iota(jnp.int32, (16, CHUNK), 1)
    source = lax.broadcasted_iota(jnp.int32, (16, CHUNK), 0)
    pick = jnp.where((feature >= 24 * source) & (feature < 24 * source + 24), 1.0, 0.0)
    flat = gfull[...].reshape(256, 128).astype(BF16)
    wide = jnp.dot(flat, spread, preferred_element_type=F32)
    return jnp.sum(wide.reshape(16, 16, CHUNK) * pick[None], axis=1)


def columns(j):
    return pl.ds(pl.multiple_of(j * CHUNK, 128), CHUNK)


def statistics(tok, mean, inverse, first, count):
    def rows(i, carry):
        at = pl.ds(pl.multiple_of(i * 16, 16), 16)
        values = tok[at, :].astype(F32)
        average = jnp.mean(values, axis=-1, keepdims=True)
        centred = values - average
        spread = jnp.mean(centred * centred, axis=-1, keepdims=True)
        mean[at, :] = average
        inverse[at, :] = lax.rsqrt(spread + EPS_NORM)
        return carry

    lax.fori_loop(first, first + count, rows, 0)


def scale_tokens(tok, gains, mean, inverse, c):
    def chunk(i, carry):
        j = i * 2 + c
        at = columns(j)
        standard = (tok[:, at].astype(F32) - mean[...]) * inverse[...]
        tok[:, at] = (standard * gains[pl.ds(j, 1), :]).astype(BF16)
        return carry

    lax.fori_loop(0, 8, chunk, 0)


def project(tok, cot, full, proj, c, first):
    at = [columns(i * 2 + c) for i in range(8)]
    low = full[:, :, :, c].reshape(8 * CHUNK, 4 * HEAD)
    inner = jnp.dot(jnp.concatenate([tok[:, a] for a in at], 1), low[:, : 3 * HEAD], preferred_element_type=F32)
    outer = jnp.dot(jnp.concatenate([cot[:, a] for a in at], 1), low[:, 3 * HEAD :], preferred_element_type=F32)
    if not first:
        inner, outer = inner + proj[:, : 3 * HEAD], outer + proj[:, 3 * HEAD :]
    proj[:, : 3 * HEAD] = inner
    proj[:, 3 * HEAD :] = outer


def normalize(values):
    average = jnp.mean(values, axis=-1, keepdims=True)
    centred = values - average
    inverse = lax.rsqrt(jnp.mean(centred * centred, axis=-1, keepdims=True) + EPS_NORM)
    return (centred * inverse, inverse)


def norm_back(grad_hat, normed, inverse):
    first_part = jnp.mean(grad_hat, axis=-1, keepdims=True)
    second_part = normed * jnp.mean(grad_hat * normed, axis=-1, keepdims=True)
    return inverse * (grad_hat - first_part - second_part)


def dot(left, right, dims):
    return lax.dot_general(left, right, (((dims[0],), (dims[1],)), ((), ())), preferred_element_type=F32)


def attend(proj, gproj):
    scaling = HEAD ** (-0.5)
    for image in range(ROWS // IMG_TOK):
        at = pl.ds(image * IMG_TOK, IMG_TOK)
        query_hat, query_inverse = normalize(proj[at, :HEAD])
        key_hat, key_inverse = normalize(proj[at, HEAD : 2 * HEAD])
        query_low, key_low = query_hat.astype(BF16), key_hat.astype(BF16)
        value_low = proj[at, 2 * HEAD : 3 * HEAD].astype(BF16)
        grad_attended = proj[at, 3 * HEAD :].astype(BF16)
        exponent = jnp.exp(dot(query_low, key_low, (1, 1)) * scaling)
        attention = exponent / jnp.sum(exponent, axis=-1, keepdims=True)
        attention_low = attention.astype(BF16)
        gproj[at, 3 * HEAD :] = dot(attention_low, value_low, (1, 0)).astype(BF16)
        gproj[at, 2 * HEAD : 3 * HEAD] = dot(attention_low, grad_attended, (0, 0)).astype(BF16)
        grad_attention = dot(grad_attended, value_low, (1, 1))
        row_total = jnp.sum(attention * grad_attention, axis=-1, keepdims=True)
        grad_scores = (attention * (grad_attention - row_total) * scaling).astype(BF16)
        grad_query_hat = dot(grad_scores, key_low, (1, 0))
        grad_key_hat = dot(grad_scores, query_low, (0, 0))
        gproj[at, :HEAD] = norm_back(grad_query_hat, query_hat, query_inverse).astype(BF16)
        gproj[at, HEAD : 2 * HEAD] = norm_back(grad_key_hat, key_hat, key_inverse).astype(BF16)


def scatter(me, mail, tok, cot, gproj, acc, sib_out, sib_in, nout, nin, fsum, fout, fin_ab, fin_c, sems):
    bs, br, ns, nr, fs, fr = sems

    def terms(yh, c):
        at = [columns((yh * 4 + i) * 2 + c) for i in range(4)]
        inner = dot(turned[: 3 * HEAD], jnp.concatenate([tok[:, a] for a in at], 1), (1, 0))
        outer = dot(turned[3 * HEAD :], jnp.concatenate([cot[:, a] for a in at], 1), (1, 0))
        return jnp.concatenate([inner, outer], 0).T.reshape(2, 2, 4, 2, 48, 4 * HEAD)

    turned = gproj[...].T
    sib = []
    for yh in range(2):
        sib_out[yh] = terms(yh, 1 - me.c).astype(BF16)
        sib.append(mail.push(sib_out.at[yh], sib_in.at[yh], bs.at[yh], br.at[yh], me.sibling()))

    def combos(stage, p):
        order = ORDERS[p][::-1]
        axis, rest, gone = order[stage], order[stage + 1:], order[:stage]
        found = []
        for n in range(2 ** len(rest)):
            found.append({a: (n >> i) & 1 for i, a in enumerate(rest)} | {a: me.low[a] for a in gone})
        return axis, found

    base = (0, 4, 6)

    def near(stage, p, yh, way):
        axis, found = combos(stage, p)
        zfar = pl.ds(2 * way, 2)
        for n, at in enumerate(found):
            yl, xl, zl = ((1 - me.low[a]) if a == axis else at[a] for a in "yxz")
            nout[p, yh, base[stage] + n, zfar] = acc[yh, yl, xl, zfar, zl, pl.ds(16 * p, 16), :].astype(BF16)
        where = (p, yh, pl.ds(base[stage], len(found)), zfar)
        k = ((stage * 3 + p) * 2 + yh) * 2 + way
        return mail.push(nout.at[where], nin.at[where], ns.at[k], nr.at[k], me.step(axis, 1 - 2 * way))

    def near_add(stage, p, yh, way):
        axis, found = combos(stage, p)
        zfar = pl.ds(2 * way, 2)
        for n, at in enumerate(found):
            yl, xl, zl = (me.low[a] if a == axis else at[a] for a in "yxz")
            place = (yh, yl, xl, zfar, zl, pl.ds(16 * p, 16), slice(None))
            acc[place] = acc[place] + nin[p, yh, base[stage] + n, zfar].astype(F32)

    flight = {}
    for yh in range(2):
        acc[yh] = terms(yh, me.c)
        sib[yh].wait_recv()
        acc[yh] = acc[yh] + sib_in[yh].astype(F32)
        for p in range(3):
            for way in range(2):
                flight[p, yh, way] = near(0, p, yh, way)
    for stage in range(3):
        for yh in range(2):
            for p in range(3):
                for way in range(2):
                    flight[p, yh, way].wait_recv()
                    near_add(stage, p, yh, way)
                    if stage < 2:
                        flight[p, yh, way] = near(stage + 1, p, yh, way)

    for yh in range(2):
        for zf in range(4):
            block = acc[yh, me.yl, me.xl, zf, me.zl]
            for xh in range(2):
                rows = block[24 * xh : 24 * xh + 24]
                rows = jnp.concatenate([rows[:, :256], rows[:, 256:]], 0)
                fsum[yh, zf, xh] = rows
                fout[yh, zf, xh] = rows.astype(BF16)
    early, late = [], []
    for k, f in enumerate(FAR_XY):
        yh, zf, xh, to = me.far(f)
        early.append(mail.push(fout.at[yh, :, xh, EARLY], fin_ab.at[k], fs.at[k], fr.at[k], to))
    for k, f in enumerate(FAR_Z):
        yh, zf, xh, to = me.far(f)
        late.append(mail.push(fout.at[:, zf, :, LATE], fin_c.at[k], fs.at[3 + k], fr.at[3 + k], to))
    for k in range(3):
        early[k].wait_recv()
        fsum[me.yh, :, me.xh, EARLY] += fin_ab[k].astype(F32)
    fout[me.yh, :, me.xh, EARLY] = fsum[me.yh, :, me.xh, EARLY].astype(BF16)
    copies = []
    for k, f in enumerate(FAR_Z):
        yh, zf, xh, to = me.far(f)
        copies.append(
            mail.push(fout.at[me.yh, zf, me.xh, EARLY], fin_ab.at[3, k], fs.at[6 + k], fr.at[6 + k], to)
        )
    for k in range(3):
        late[k].wait_recv()
        fsum[:, me.zf, :, LATE] += fin_c[k].astype(F32)
    fout[:, me.zf, :, LATE] = fsum[:, me.zf, :, LATE].astype(BF16)
    for k, f in enumerate(FAR_XY):
        yh, zf, xh, to = me.far(f)
        copies.append(
            mail.push(fout.at[yh, me.zf, xh, LATE], fin_c.at[3, k // 2, k % 2], fs.at[9 + k], fr.at[9 + k], to)
        )
    total_ab = fsum[me.yh, me.zf, me.xh, EARLY]
    total_c = fsum[me.yh, me.zf, me.xh, LATE]
    for k in range(3):
        copies[k].wait_recv()
        total_ab = total_ab + fin_ab[3, k].astype(F32)
    for k in range(3):
        copies[3 + k].wait_recv()
        total_c = total_c + fin_c[3, k // 2, k % 2].astype(F32)
    total = jnp.concatenate([total_ab, total_c], 0)
    return jnp.concatenate([total[:24], total[24:]], 1)


def adam_step(parameter, moment_one, moment_two, gradient, decay_rate):
    fresh_one = BETA_ONE * moment_one + (1.0 - BETA_ONE) * gradient
    fresh_two = BETA_TWO * moment_two + (1.0 - BETA_TWO) * gradient * gradient
    adjusted = fresh_one / CORRECT_ONE / (jnp.sqrt(fresh_two / CORRECT_TWO) + ADAM_EPS)
    return (parameter - LEARN_RATE * (adjusted + decay_rate * parameter), fresh_one, fresh_two)


def stacked(rows):
    return jnp.concatenate([rows[:, :256], rows[:, 256:]], 0).astype(BF16)


def gain_line(place, row):
    place[...] = jnp.zeros((1, 128), F32)
    place[:, :24] = row.astype(BF16).astype(F32)


def as_row(column):
    lane = lax.broadcasted_iota(jnp.int32, (24, 24), 1)
    row = lax.broadcasted_iota(jnp.int32, (24, 24), 0)
    return jnp.sum(jnp.where(lane == row, column, 0.0), axis=0, keepdims=True)


def whole(
    tokens, cotangent, weights, first, second, gain, gain_one, gain_two,
    new_weights, new_first, new_second, new_gain, new_gain_one, new_gain_two, next_weights, next_gain,
    tok, cot, full, full_two, gfull, gnext, land, land_two, shard, gains, mean, inverse, proj, gproj,
    acc, sib_out, sib_in, nout, nin, fsum, fout, fin_ab, fin_c, small, load, rsem, *sems
):
    me = Place()
    mail = Mail()
    loads = [pltpu.make_async_copy(tokens, tok, load.at[0]), pltpu.make_async_copy(cotangent, cot, load.at[1])]
    for copy in loads:
        copy.start()
    shard[...] = stacked(weights[...])
    gain_line(gfull.at[me.yh, me.yl, me.xl, me.c, me.zf, me.zl, me.xh], gain[...])
    enter(me)

    def far_one():
        loads[0].wait()
        statistics(tok, mean, inverse, 0, 14)

    def far_two():
        statistics(tok, mean, inverse, 14, 10)

    def near_one():
        statistics(tok, mean, inverse, 24, 8)

    def gains_here(shared):
        shared.wait_recv()
        gains[...] = gain_rows(gfull)
        scale_tokens(tok, gains, mean, inverse, me.c)
        loads[1].wait()

    def scale_here():
        scale_tokens(tok, gains, mean, inverse, 1 - me.c)

    def own_here():
        project(tok, cot, full, proj, me.c, True)

    nothing = lambda: None
    gather(
        me, mail, shard, full, gfull, land, sems[:8],
        (far_one, far_two, near_one, nothing, nothing, gains_here, scale_here, own_here),
    )
    project(tok, cot, full, proj, 1 - me.c, False)
    attend(proj, gproj)
    gradient = scatter(
        me, mail, tok, cot, gproj, acc, sib_out, sib_in, nout, nin, fsum, fout, fin_ab, fin_c, sems[16:]
    )
    low = weights[:, : 3 * HEAD].astype(BF16).astype(F32)
    grad_gain = as_row(jnp.sum(gradient[:, : 3 * HEAD] * low, axis=1, keepdims=True))
    grad_gain = grad_gain / gain[...].astype(BF16).astype(F32)
    fresh, one, two = adam_step(weights[...], first[...], second[...], gradient, DECAY_RATE)
    saves = []
    for k, (value, to) in enumerate(((fresh, new_weights), (one, new_first), (two, new_second))):
        small[k] = value
        saves.append(pltpu.make_async_copy(small.at[k], to, load.at[2 + k]))
        saves[-1].start()
    fresh_gain, one, two = adam_step(gain[...], gain_one[...], gain_two[...], grad_gain, 0.0)
    new_gain[...], new_gain_one[...], new_gain_two[...] = fresh_gain, one, two
    shard[...] = stacked(fresh)
    gain_line(gnext.at[me.yh, me.yl, me.xl, me.c, me.zf, me.zl, me.xh], fresh_gain)

    def next_here(shared):
        shared.wait_recv()
        next_gain[...] = gain_rows(gnext)

    gather(
        me, mail, shard, full_two, gnext, land_two, sems[8:16], (nothing,) * 5 + (next_here, nothing, nothing),
        next_weights, rsem,
    )
    for copy in saves:
        copy.wait()
    mail.close()


def keep(*refs):
    count = (len(refs) - 2) // 3
    here, there, held, came, left = refs[:count], refs[count : 2 * count], refs[2 * count : 3 * count], refs[-2], refs[-1]
    pairs = []
    for i in range(count):
        if len(here[i].shape) > 2:
            for n in range(8):
                at = (n // 4, n // 2 % 2, n % 2)
                pairs.append((here[i].at[at], held[i].at[at], there[i].at[at]))
        else:
            pairs.append((here[i], held[i], there[i]))
    ins = [pltpu.make_async_copy(a, b, came.at[k]) for k, (a, b, c) in enumerate(pairs)]
    outs = [pltpu.make_async_copy(b, c, left.at[k]) for k, (a, b, c) in enumerate(pairs)]
    for copy in ins:
        copy.start()
    for a, b in zip(ins, outs):
        a.wait()
        b.start()
    for copy in outs:
        copy.wait()


def shards(
    tokens, cotangent, weights, first_moment, second_moment, norm_gain, gain_first, gain_second
):
    dma, vmem = pltpu.SemaphoreType.DMA, pltpu.VMEM
    own, line = jax.ShapeDtypeStruct((24, 512), F32), jax.ShapeDtypeStruct((1, 24), F32)
    gather_sems = [dma((12,))] * 2 + [dma((9,))] * 2 + [dma((36,))] * 2 + [dma((14,))] * 2
    out = pl.pallas_call(
        whole,
        name="whole",
        out_shape=(own,) * 3 + (line,) * 3
        + (jax.ShapeDtypeStruct(VIEW, BF16), jax.ShapeDtypeStruct((16, CHUNK), F32)),
        in_specs=[pl.BlockSpec(memory_space=pl.ANY)] * 2 + [pl.BlockSpec(memory_space=pltpu.VMEM)] * 6,
        out_specs=(pl.BlockSpec(memory_space=pl.ANY),) * 3 + (pl.BlockSpec(memory_space=pltpu.VMEM),) * 3
        + (pl.BlockSpec(memory_space=pl.ANY), pl.BlockSpec(memory_space=pltpu.VMEM)),
        scratch_shapes=[
            vmem((ROWS, 6144), BF16),
            vmem((ROWS, 6144), BF16),
            vmem(VIEW, BF16),
            vmem(VIEW, BF16),
            vmem(GVIEW, F32),
            vmem(GVIEW, F32),
            vmem((2, 4, 2, 48, 256), BF16),
            vmem((2, 4, 2, 48, 256), BF16),
            vmem((48, 256), BF16),
            vmem((16, CHUNK), F32),
            vmem((ROWS, 1), F32),
            vmem((ROWS, 1), F32),
            vmem((ROWS, 4 * HEAD), F32),
            vmem((ROWS, 4 * HEAD), BF16),
            vmem((2, 2, 2, 4, 2, 48, 512), F32),
            vmem((2, 2, 2, 4, 2, 48, 512), BF16),
            vmem((2, 2, 2, 4, 2, 48, 512), BF16),
            vmem((3, 2, 7, 4, 16, 512), BF16),
            vmem((3, 2, 7, 4, 16, 512), BF16),
            vmem((2, 4, 2, 48, 256), F32),
            vmem((2, 4, 2, 48, 256), BF16),
            vmem((4, 4, 32, 256), BF16),
            vmem((4, 2, 2, 16, 256), BF16),
            vmem((3, 24, 512), F32),
            dma((5,)),
            dma((14,)),
        ] + gather_sems * 2 + [dma((2,))] * 2 + [dma((36,))] * 2 + [dma((12,))] * 2,
        compiler_params=pltpu.CompilerParams(
            collective_id=1, has_side_effects=True, vmem_limit_bytes=56 << 20
        ),
    )(
        tokens, cotangent, weights, first_moment, second_moment,
        norm_gain.reshape(1, 24), gain_first.reshape(1, 24), gain_second.reshape(1, 24),
    )
    kept = (0, 1, 2, 3, 4, 5, 6)
    copies = pl.pallas_call(
        keep,
        name="keep",
        out_shape=tuple(jax.ShapeDtypeStruct(out[i].shape, out[i].dtype) for i in kept),
        in_specs=[pl.BlockSpec(memory_space=pl.ANY)] * len(kept),
        out_specs=(pl.BlockSpec(memory_space=pl.ANY),) * len(kept),
        scratch_shapes=[vmem(out[i].shape, out[i].dtype) for i in kept] + [dma((len(kept) + 7,))] * 2,
        compiler_params=pltpu.CompilerParams(vmem_limit_bytes=60 << 20),
    )(*(out[i] for i in kept))
    return (
        *copies[:3],
        *(copy.reshape(24) for copy in copies[3:6]),
        copies[6].reshape(6144, 512),
        out[7].reshape(6144).astype(BF16),
    )


def solution(mesh):
    rows, line = P(("gx", "gy"), None), P(("gx", "gy"))
    return jax.shard_map(
        shards,
        mesh=mesh,
        in_specs=(rows,) * 5 + (line,) * 3,
        out_specs=(rows,) * 3 + (line,) * 3 + (P(), P()),
        check_vma=False,
    )
```

```python
import functools

import jax
import jax.numpy as jnp
from jax import lax
from jax.experimental import pallas as pl
from jax.experimental.pallas import tpu as pltpu
from jax.sharding import PartitionSpec as P

IMG_TOK = 256
EPS_NORM = 1e-06
BETA_ONE = 0.9
BETA_TWO = 0.95
LEARN_RATE = 0.001
DECAY_RATE = 0.1
ADAM_EPS = 1e-08
CORRECT_ONE = 1.0 - 0.9**10
CORRECT_TWO = 1.0 - 0.95**10
MESH = pl.DeviceIdType.MESH
BF16, F32 = jnp.bfloat16, jnp.float32

VIEW = (2, 2, 2, 2, 4, 2, 48, 512)
GVIEW = (2, 2, 2, 2, 4, 2, 2, 1, 128)
ROWS, HEAD, CHUNK = 512, 128, 384
FAR_Z = [(0, dz, 0) for dz in (1, 3, 2)]
FAR_XY = [(0, 0, 1), (1, 0, 0), (1, 0, 1)]
EARLY, LATE = pl.ds(0, 32), pl.ds(32, 16)
ORDERS = (("z", "y", "x"), ("x", "z", "y"), ("y", "x", "z"))


class Place:
    def __init__(self):
        gx, gy = lax.axis_index("gx"), lax.axis_index("gy")
        self.y, self.z = gx // 4, gy // 2
        self.xl, self.c, self.xh = lax.rem(gx // 2, 2), lax.rem(gx, 2), lax.rem(gy, 2)
        self.yh, self.yl, self.zf, self.zl = self.y // 2, lax.rem(self.y, 2), self.z // 2, lax.rem(self.z, 2)
        self.x = self.xh * 2 + self.xl
        self.low = {"x": self.xl, "y": self.yl, "z": self.zl}

    def device(self, x, y, z, c):
        return (y * 4 + lax.rem(x, 2) * 2 + c, z * 2 + x // 2)

    def step(self, axis, by):
        x, y, z = self.x, self.y, self.z
        if axis == "x":
            x = lax.rem(x + by + 4, 4)
        elif axis == "y":
            y = lax.rem(y + by + 4, 4)
        else:
            z = lax.rem(z + by + 8, 8)
        return self.device(x, y, z, self.c)

    def sibling(self):
        return self.device(self.x, self.y, self.z, 1 - self.c)

    def far(self, offset):
        dy, dz, dx = offset
        yh, zf, xh = lax.rem(self.yh + dy, 2), lax.rem(self.zf + dz, 4), lax.rem(self.xh + dx, 2)
        return yh, zf, xh, self.device(xh * 2 + self.xl, yh * 2 + self.yl, zf * 2 + self.zl, self.c)


def enter(me):
    barrier = pltpu.get_barrier_semaphore()
    others = [me.far(f)[3] for f in FAR_Z + FAR_XY] + [me.step(a, b) for a in "xyz" for b in (1, -1)] + [me.sibling()]
    for other in others:
        pl.semaphore_signal(barrier, inc=1, device_id=other, device_id_type=MESH)
    pl.semaphore_wait(barrier, len(others))


class Mail:
    def __init__(self):
        self.sends = []

    def push(self, src, dst, ssem, rsem, to):
        copy = pltpu.make_async_remote_copy(src, dst, ssem, rsem, device_id=to, device_id_type=MESH)
        copy.start()
        self.sends.append(copy)
        return copy

    def close(self):
        for copy in self.sends:
            copy.wait_send()


def gather(me, mail, shard, full, gfull, land, sems, between, result=None, rsem=None):
    fs, fr, gs, gr, ns, nr, ss, sr = sems
    yh, zf, xh = me.yh, me.zf, me.xh
    land[yh, zf, xh] = shard[...]

    def far(first, src_z, src_xy):
        copies = []
        for group, src in ((FAR_Z, src_z), (FAR_XY, src_xy)):
            for f in group:
                k = first + len(copies)
                copies.append(mail.push(src, src, fs.at[k], fr.at[k], me.far(f)[3]))
        return copies

    def far_gain(first, group, src):
        return [
            mail.push(src, src, gs.at[first + k], gr.at[first + k], me.far(f)[3]) for k, f in enumerate(group)
        ]

    own_gain = gfull.at[:, me.yl, me.xl, me.c, :, me.zl]
    gains = far_gain(0, FAR_Z, own_gain.at[yh, zf, xh])
    copies = far(0, land.at[yh, zf, xh, EARLY], land.at[yh, zf, xh, LATE])
    between[0]()
    for copy in gains:
        copy.wait_recv()
    gains = far_gain(3, FAR_XY, own_gain.at[yh, :, xh])
    for copy in copies:
        copy.wait_recv()
    copies = far(6, land.at[:, zf, :, LATE], land.at[yh, :, xh, EARLY])
    between[1]()
    for copy in gains + copies:
        copy.wait_recv()

    def near_gain(stage):
        axis, done = "zyx"[stage], "zyx"[:stage]
        at = {a: (slice(None) if a in done else me.low[a]) for a in "xyz"}
        src = gfull.at[:, at["y"], at["x"], me.c, :, at["z"]]
        return mail.push(src, src, gs.at[6 + stage], gr.at[6 + stage], me.step(axis, 1))

    gflight = near_gain(0)
    for h in range(2):
        for f in range(4):
            a, b = (land[h, f, g].astype(F32) for g in range(2))
            block = jnp.concatenate(
                [jnp.concatenate([a[:24], b[:24]], 0), jnp.concatenate([a[24:], b[24:]], 0)], 1
            )
            full[h, me.yl, me.xl, me.c, f, me.zl] = block.astype(BF16)

    def part(ref, done, half, zfar, p, fresh=None):
        at = {a: (slice(None) if a in done else me.low[a]) for a in "xyz"}
        if fresh is not None:
            at[fresh] = 1 - me.low[fresh]
        return ref.at[half, at["y"], at["x"], me.c, zfar, at["z"], pl.ds(16 * p, 16)]

    shared, local = [], []

    def share(view, src):
        k = len(shared)
        to = src if result is None else result
        shared.append(mail.push(view(src), view(to), ss.at[k], sr.at[k], me.sibling()))
        if result is not None:
            local.append(pltpu.make_async_copy(view(src), view(result), rsem.at[k]))
            local[-1].start()

    both = slice(None)
    flight = {}

    def near(stage, q):
        for p in range(3):
            axis, done = ORDERS[p][stage], ORDERS[p][:stage]
            for half in range(2):
                if stage > 0:
                    flight[stage - 1, p, half, q].wait_recv()
                src = part(full, done, half, pl.ds(2 * q, 2), p)
                k = ((stage * 3 + p) * 2 + half) * 2 + q
                flight[stage, p, half, q] = mail.push(src, src, ns.at[k], nr.at[k], me.step(axis, 1 - 2 * half))

    def spread_news(stage, zfar, parts=(0, 1, 2)):
        for p in parts:
            share(lambda ref: part(ref, ORDERS[p][:stage], both, zfar, p, ORDERS[p][stage]), full)

    near(0, 0)
    near(0, 1)
    share(lambda ref: ref.at[:, me.yl, me.xl, me.c, :, me.zl], full)
    between[2]()
    for stage in (1, 2):
        gflight.wait_recv()
        gflight = near_gain(stage)
        near(stage, 0)
        near(stage, 1)
        spread_news(stage - 1, both)
        between[2 + stage]()
    gflight.wait_recv()
    place = gfull.at[:, :, :, me.c]
    shared.append(mail.push(place, place, ss.at[7], sr.at[7], me.sibling()))
    between[5](shared[-1])
    for q in range(2):
        for p in range(3):
            for half in range(2):
                flight[2, p, half, q].wait_recv()
            spread_news(2, pl.ds(2 * q, 2), (p,))
        between[6 + q]()
    for k, copy in enumerate(shared):
        if k != 7:
            copy.wait_recv()
    for copy in local:
        copy.wait()


def gain_rows(gfull):
    feature = lax.broadcasted_iota(jnp.int32, (128, CHUNK), 1).astype(F32)
    lane = lax.broadcasted_iota(jnp.int32, (128, CHUNK), 0).astype(F32)
    spread = jnp.where(feature - 24.0 * jnp.floor((feature + 0.5) * (1.0 / 24.0)) == lane, 1.0, 0.0).astype(BF16)
    feature = lax.broadcasted_iota(jnp.int32, (16, CHUNK), 1)
    source = lax.broadcasted_iota(jnp.int32, (16, CHUNK), 0)
    pick = jnp.where((feature >= 24 * source) & (feature < 24 * source + 24), 1.0, 0.0)
    flat = gfull[...].reshape(256, 128).astype(BF16)
    wide = jnp.dot(flat, spread, preferred_element_type=F32)
    return jnp.sum(wide.reshape(16, 16, CHUNK) * pick[None], axis=1)


def columns(j):
    return pl.ds(pl.multiple_of(j * CHUNK, 128), CHUNK)


def statistics(tok, mean, inverse, first, count):
    def rows(i, carry):
        at = pl.ds(pl.multiple_of(i * 16, 16), 16)
        values = tok[at, :].astype(F32)
        average = jnp.mean(values, axis=-1, keepdims=True)
        centred = values - average
        spread = jnp.mean(centred * centred, axis=-1, keepdims=True)
        mean[at, :] = average
        inverse[at, :] = lax.rsqrt(spread + EPS_NORM)
        return carry

    lax.fori_loop(first, first + count, rows, 0)


def scale_tokens(tok, gains, mean, inverse, c):
    def chunk(i, carry):
        j = i * 2 + c
        at = columns(j)
        standard = (tok[:, at].astype(F32) - mean[...]) * inverse[...]
        tok[:, at] = (standard * gains[pl.ds(j, 1), :]).astype(BF16)
        return carry

    lax.fori_loop(0, 8, chunk, 0)


def project(tok, cot, full, proj, c, first):
    at = [columns(i * 2 + c) for i in range(8)]
    low = full[:, :, :, c].reshape(8 * CHUNK, 4 * HEAD)
    inner = jnp.dot(jnp.concatenate([tok[:, a] for a in at], 1), low[:, : 3 * HEAD], preferred_element_type=F32)
    outer = jnp.dot(jnp.concatenate([cot[:, a] for a in at], 1), low[:, 3 * HEAD :], preferred_element_type=F32)
    if not first:
        inner, outer = inner + proj[:, : 3 * HEAD], outer + proj[:, 3 * HEAD :]
    proj[:, : 3 * HEAD] = inner
    proj[:, 3 * HEAD :] = outer


def normalize(values):
    average = jnp.mean(values, axis=-1, keepdims=True)
    centred = values - average
    inverse = lax.rsqrt(jnp.mean(centred * centred, axis=-1, keepdims=True) + EPS_NORM)
    return (centred * inverse, inverse)


def norm_back(grad_hat, normed, inverse):
    first_part = jnp.mean(grad_hat, axis=-1, keepdims=True)
    second_part = normed * jnp.mean(grad_hat * normed, axis=-1, keepdims=True)
    return inverse * (grad_hat - first_part - second_part)


def dot(left, right, dims):
    return lax.dot_general(left, right, (((dims[0],), (dims[1],)), ((), ())), preferred_element_type=F32)


def attend(proj, gproj):
    scaling = HEAD ** (-0.5)
    for image in range(ROWS // IMG_TOK):
        at = pl.ds(image * IMG_TOK, IMG_TOK)
        query_hat, query_inverse = normalize(proj[at, :HEAD])
        key_hat, key_inverse = normalize(proj[at, HEAD : 2 * HEAD])
        query_low, key_low = query_hat.astype(BF16), key_hat.astype(BF16)
        value_low = proj[at, 2 * HEAD : 3 * HEAD].astype(BF16)
        grad_attended = proj[at, 3 * HEAD :].astype(BF16)
        exponent = jnp.exp(dot(query_low, key_low, (1, 1)) * scaling)
        attention = exponent / jnp.sum(exponent, axis=-1, keepdims=True)
        attention_low = attention.astype(BF16)
        gproj[at, 3 * HEAD :] = dot(attention_low, value_low, (1, 0)).astype(BF16)
        gproj[at, 2 * HEAD : 3 * HEAD] = dot(attention_low, grad_attended, (0, 0)).astype(BF16)
        grad_attention = dot(grad_attended, value_low, (1, 1))
        row_total = jnp.sum(attention * grad_attention, axis=-1, keepdims=True)
        grad_scores = (attention * (grad_attention - row_total) * scaling).astype(BF16)
        grad_query_hat = dot(grad_scores, key_low, (1, 0))
        grad_key_hat = dot(grad_scores, query_low, (0, 0))
        gproj[at, :HEAD] = norm_back(grad_query_hat, query_hat, query_inverse).astype(BF16)
        gproj[at, HEAD : 2 * HEAD] = norm_back(grad_key_hat, key_hat, key_inverse).astype(BF16)


def scatter(me, mail, tok, cot, gproj, acc, sib_out, sib_in, nout, nin, fsum, fout, fin_ab, fin_c, sems):
    bs, br, ns, nr, fs, fr = sems

    def terms(yh, c):
        at = [columns((yh * 4 + i) * 2 + c) for i in range(4)]
        inner = dot(turned[: 3 * HEAD], jnp.concatenate([tok[:, a] for a in at], 1), (1, 0))
        outer = dot(turned[3 * HEAD :], jnp.concatenate([cot[:, a] for a in at], 1), (1, 0))
        return jnp.concatenate([inner, outer], 0).T.reshape(2, 2, 4, 2, 48, 4 * HEAD)

    turned = gproj[...].T
    sib = []
    for yh in range(2):
        sib_out[yh] = terms(yh, 1 - me.c).astype(BF16)
        sib.append(mail.push(sib_out.at[yh], sib_in.at[yh], bs.at[yh], br.at[yh], me.sibling()))

    def combos(stage, p):
        order = ORDERS[p][::-1]
        axis, rest, gone = order[stage], order[stage + 1:], order[:stage]
        found = []
        for n in range(2 ** len(rest)):
            found.append({a: (n >> i) & 1 for i, a in enumerate(rest)} | {a: me.low[a] for a in gone})
        return axis, found

    base = (0, 4, 6)

    def near(stage, p, yh, way):
        axis, found = combos(stage, p)
        zfar = pl.ds(2 * way, 2)
        for n, at in enumerate(found):
            yl, xl, zl = ((1 - me.low[a]) if a == axis else at[a] for a in "yxz")
            nout[p, yh, base[stage] + n, zfar] = acc[yh, yl, xl, zfar, zl, pl.ds(16 * p, 16), :].astype(BF16)
        where = (p, yh, pl.ds(base[stage], len(found)), zfar)
        k = ((stage * 3 + p) * 2 + yh) * 2 + way
        return mail.push(nout.at[where], nin.at[where], ns.at[k], nr.at[k], me.step(axis, 1 - 2 * way))

    def near_add(stage, p, yh, way):
        axis, found = combos(stage, p)
        zfar = pl.ds(2 * way, 2)
        for n, at in enumerate(found):
            yl, xl, zl = (me.low[a] if a == axis else at[a] for a in "yxz")
            place = (yh, yl, xl, zfar, zl, pl.ds(16 * p, 16), slice(None))
            acc[place] = acc[place] + nin[p, yh, base[stage] + n, zfar].astype(F32)

    flight = {}
    for yh in range(2):
        acc[yh] = terms(yh, me.c)
        sib[yh].wait_recv()
        acc[yh] = acc[yh] + sib_in[yh].astype(F32)
        for p in range(3):
            for way in range(2):
                flight[p, yh, way] = near(0, p, yh, way)
    for stage in range(3):
        for yh in range(2):
            for p in range(3):
                for way in range(2):
                    flight[p, yh, way].wait_recv()
                    near_add(stage, p, yh, way)
                    if stage < 2:
                        flight[p, yh, way] = near(stage + 1, p, yh, way)

    for yh in range(2):
        for zf in range(4):
            block = acc[yh, me.yl, me.xl, zf, me.zl]
            for xh in range(2):
                rows = block[24 * xh : 24 * xh + 24]
                rows = jnp.concatenate([rows[:, :256], rows[:, 256:]], 0)
                fsum[yh, zf, xh] = rows
                fout[yh, zf, xh] = rows.astype(BF16)
    early, late = [], []
    for k, f in enumerate(FAR_XY):
        yh, zf, xh, to = me.far(f)
        early.append(mail.push(fout.at[yh, :, xh, EARLY], fin_ab.at[k], fs.at[k], fr.at[k], to))
    for k, f in enumerate(FAR_Z):
        yh, zf, xh, to = me.far(f)
        late.append(mail.push(fout.at[:, zf, :, LATE], fin_c.at[k], fs.at[3 + k], fr.at[3 + k], to))
    for k in range(3):
        early[k].wait_recv()
        fsum[me.yh, :, me.xh, EARLY] += fin_ab[k].astype(F32)
    fout[me.yh, :, me.xh, EARLY] = fsum[me.yh, :, me.xh, EARLY].astype(BF16)
    copies = []
    for k, f in enumerate(FAR_Z):
        yh, zf, xh, to = me.far(f)
        copies.append(
            mail.push(fout.at[me.yh, zf, me.xh, EARLY], fin_ab.at[3, k], fs.at[6 + k], fr.at[6 + k], to)
        )
    for k in range(3):
        late[k].wait_recv()
        fsum[:, me.zf, :, LATE] += fin_c[k].astype(F32)
    fout[:, me.zf, :, LATE] = fsum[:, me.zf, :, LATE].astype(BF16)
    for k, f in enumerate(FAR_XY):
        yh, zf, xh, to = me.far(f)
        copies.append(
            mail.push(fout.at[yh, me.zf, xh, LATE], fin_c.at[3, k // 2, k % 2], fs.at[9 + k], fr.at[9 + k], to)
        )
    total_ab = fsum[me.yh, me.zf, me.xh, EARLY]
    total_c = fsum[me.yh, me.zf, me.xh, LATE]
    for k in range(3):
        copies[k].wait_recv()
        total_ab = total_ab + fin_ab[3, k].astype(F32)
    for k in range(3):
        copies[3 + k].wait_recv()
        total_c = total_c + fin_c[3, k // 2, k % 2].astype(F32)
    total = jnp.concatenate([total_ab, total_c], 0)
    return jnp.concatenate([total[:24], total[24:]], 1)


def adam_step(parameter, moment_one, moment_two, gradient, decay_rate):
    fresh_one = BETA_ONE * moment_one + (1.0 - BETA_ONE) * gradient
    fresh_two = BETA_TWO * moment_two + (1.0 - BETA_TWO) * gradient * gradient
    adjusted = fresh_one / CORRECT_ONE / (jnp.sqrt(fresh_two / CORRECT_TWO) + ADAM_EPS)
    return (parameter - LEARN_RATE * (adjusted + decay_rate * parameter), fresh_one, fresh_two)


def stacked(rows):
    return jnp.concatenate([rows[:, :256], rows[:, 256:]], 0).astype(BF16)


def gain_line(place, row):
    place[...] = jnp.zeros((1, 128), F32)
    place[:, :24] = row.astype(BF16).astype(F32)


def as_row(column):
    lane = lax.broadcasted_iota(jnp.int32, (24, 24), 1)
    row = lax.broadcasted_iota(jnp.int32, (24, 24), 0)
    return jnp.sum(jnp.where(lane == row, column, 0.0), axis=0, keepdims=True)


def whole(
    tokens, cotangent, weights, first, second, gain, gain_one, gain_two,
    new_weights, new_first, new_second, new_gain, new_gain_one, new_gain_two, next_weights, next_gain,
    tok, cot, full, full_two, gfull, gnext, land, land_two, shard, gains, mean, inverse, proj, gproj,
    acc, sib_out, sib_in, nout, nin, fsum, fout, fin_ab, fin_c, small, load, rsem, *sems
):
    me = Place()
    mail = Mail()
    loads = [pltpu.make_async_copy(tokens, tok, load.at[0]), pltpu.make_async_copy(cotangent, cot, load.at[1])]
    for copy in loads:
        copy.start()
    shard[...] = stacked(weights[...])
    gain_line(gfull.at[me.yh, me.yl, me.xl, me.c, me.zf, me.zl, me.xh], gain[...])
    enter(me)

    def far_one():
        loads[0].wait()
        statistics(tok, mean, inverse, 0, 14)

    def far_two():
        statistics(tok, mean, inverse, 14, 10)

    def near_one():
        statistics(tok, mean, inverse, 24, 8)

    def gains_here(shared):
        shared.wait_recv()
        gains[...] = gain_rows(gfull)
        scale_tokens(tok, gains, mean, inverse, me.c)
        loads[1].wait()

    def scale_here():
        scale_tokens(tok, gains, mean, inverse, 1 - me.c)

    def own_here():
        project(tok, cot, full, proj, me.c, True)

    nothing = lambda: None
    gather(
        me, mail, shard, full, gfull, land, sems[:8],
        (far_one, far_two, near_one, nothing, nothing, gains_here, scale_here, own_here),
    )
    project(tok, cot, full, proj, 1 - me.c, False)
    attend(proj, gproj)
    gradient = scatter(
        me, mail, tok, cot, gproj, acc, sib_out, sib_in, nout, nin, fsum, fout, fin_ab, fin_c, sems[16:]
    )
    low = weights[:, : 3 * HEAD].astype(BF16).astype(F32)
    grad_gain = as_row(jnp.sum(gradient[:, : 3 * HEAD] * low, axis=1, keepdims=True))
    grad_gain = grad_gain / gain[...].astype(BF16).astype(F32)
    fresh, one, two = adam_step(weights[...], first[...], second[...], gradient, DECAY_RATE)
    saves = []
    for k, (value, to) in enumerate(((fresh, new_weights), (one, new_first), (two, new_second))):
        small[k] = value
        saves.append(pltpu.make_async_copy(small.at[k], to, load.at[2 + k]))
        saves[-1].start()
    fresh_gain, one, two = adam_step(gain[...], gain_one[...], gain_two[...], grad_gain, 0.0)
    new_gain[...], new_gain_one[...], new_gain_two[...] = fresh_gain, one, two
    shard[...] = stacked(fresh)
    gain_line(gnext.at[me.yh, me.yl, me.xl, me.c, me.zf, me.zl, me.xh], fresh_gain)

    def next_here(shared):
        shared.wait_recv()
        next_gain[...] = gain_rows(gnext)

    gather(
        me, mail, shard, full_two, gnext, land_two, sems[8:16], (nothing,) * 5 + (next_here, nothing, nothing),
        next_weights, rsem,
    )
    for copy in saves:
        copy.wait()
    mail.close()


def keep(*refs):
    count = (len(refs) - 2) // 3
    here, there, held, came, left = refs[:count], refs[count : 2 * count], refs[2 * count : 3 * count], refs[-2], refs[-1]
    pairs = []
    for i in range(count):
        if len(here[i].shape) > 2:
            for n in range(8):
                at = (n // 4, n // 2 % 2, n % 2)
                pairs.append((here[i].at[at], held[i].at[at], there[i].at[at]))
        else:
            pairs.append((here[i], held[i], there[i]))
    ins = [pltpu.make_async_copy(a, b, came.at[k]) for k, (a, b, c) in enumerate(pairs)]
    outs = [pltpu.make_async_copy(b, c, left.at[k]) for k, (a, b, c) in enumerate(pairs)]
    for copy in ins:
        copy.start()
    for a, b in zip(ins, outs):
        a.wait()
        b.start()
    for copy in outs:
        copy.wait()


def shards(
    tokens, cotangent, weights, first_moment, second_moment, norm_gain, gain_first, gain_second
):
    dma, vmem = pltpu.SemaphoreType.DMA, pltpu.VMEM
    own, line = jax.ShapeDtypeStruct((24, 512), F32), jax.ShapeDtypeStruct((1, 24), F32)
    gather_sems = [dma((12,))] * 2 + [dma((9,))] * 2 + [dma((36,))] * 2 + [dma((14,))] * 2
    out = pl.pallas_call(
        whole,
        name="whole",
        out_shape=(own,) * 3 + (line,) * 3
        + (jax.ShapeDtypeStruct(VIEW, BF16), jax.ShapeDtypeStruct((16, CHUNK), F32)),
        in_specs=[pl.BlockSpec(memory_space=pl.ANY)] * 2 + [pl.BlockSpec(memory_space=pltpu.VMEM)] * 6,
        out_specs=(pl.BlockSpec(memory_space=pl.ANY),) * 3 + (pl.BlockSpec(memory_space=pltpu.VMEM),) * 3
        + (pl.BlockSpec(memory_space=pl.ANY), pl.BlockSpec(memory_space=pltpu.VMEM)),
        scratch_shapes=[
            vmem((ROWS, 6144), BF16),
            vmem((ROWS, 6144), BF16),
            vmem(VIEW, BF16),
            vmem(VIEW, BF16),
            vmem(GVIEW, F32),
            vmem(GVIEW, F32),
            vmem((2, 4, 2, 48, 256), BF16),
            vmem((2, 4, 2, 48, 256), BF16),
            vmem((48, 256), BF16),
            vmem((16, CHUNK), F32),
            vmem((ROWS, 1), F32),
            vmem((ROWS, 1), F32),
            vmem((ROWS, 4 * HEAD), F32),
            vmem((ROWS, 4 * HEAD), BF16),
            vmem((2, 2, 2, 4, 2, 48, 512), F32),
            vmem((2, 2, 2, 4, 2, 48, 512), BF16),
            vmem((2, 2, 2, 4, 2, 48, 512), BF16),
            vmem((3, 2, 7, 4, 16, 512), BF16),
            vmem((3, 2, 7, 4, 16, 512), BF16),
            vmem((2, 4, 2, 48, 256), F32),
            vmem((2, 4, 2, 48, 256), BF16),
            vmem((4, 4, 32, 256), BF16),
            vmem((4, 2, 2, 16, 256), BF16),
            vmem((3, 24, 512), F32),
            dma((5,)),
            dma((14,)),
        ] + gather_sems * 2 + [dma((2,))] * 2 + [dma((36,))] * 2 + [dma((12,))] * 2,
        compiler_params=pltpu.CompilerParams(
            collective_id=1, has_side_effects=True, vmem_limit_bytes=56 << 20
        ),
    )(
        tokens, cotangent, weights, first_moment, second_moment,
        norm_gain.reshape(1, 24), gain_first.reshape(1, 24), gain_second.reshape(1, 24),
    )
    kept = (0, 1, 2, 3, 4, 5, 6)
    copies = pl.pallas_call(
        keep,
        name="keep",
        out_shape=tuple(jax.ShapeDtypeStruct(out[i].shape, out[i].dtype) for i in kept),
        in_specs=[pl.BlockSpec(memory_space=pl.ANY)] * len(kept),
        out_specs=(pl.BlockSpec(memory_space=pl.ANY),) * len(kept),
        scratch_shapes=[vmem(out[i].shape, out[i].dtype) for i in kept] + [dma((len(kept) + 7,))] * 2,
        compiler_params=pltpu.CompilerParams(vmem_limit_bytes=60 << 20),
    )(*(out[i] for i in kept))
    return (
        *copies[:3],
        *(copy.reshape(24) for copy in copies[3:6]),
        copies[6].reshape(6144, 512),
        out[7].reshape(6144).astype(BF16),
    )


def solution(mesh):
    rows, line = P(("gx", "gy"), None), P(("gx", "gy"))
    return jax.shard_map(
        shards,
        mesh=mesh,
        in_specs=(rows,) * 5 + (line,) * 3,
        out_specs=(rows,) * 3 + (line,) * 3 + (P(), P()),
        check_vma=False,
    )
```
